256 devices in a mesh: row: 16 (over z, y_lo), col: 16 (over x, y_hi, core).
Axes of the slice: x: 4, y: 4 (y_hi: 2, y_lo: 2; y = y_hi * 2 + y_lo), z: 8, core: 2. Of those that a mesh axis runs over, the one named last changes fastest.
Arguments:
- matrix: float32 [4096, 8192], P('row', 'col'), may hold values from -30 to 30
- shifts: int32 [2, 8], replicated, may hold values from 0 to 255
Outputs:
- rotated: float32 [4096, 8192], P('row', 'col')
The draws below stay inside these ranges and needn't reach their ends.
All inputs are finite; a program needn't handle non-finite values.
Results may differ from the reference program's by a relative error of at most 0.0003.
Values sent between devices are 32-bit elements; how exact they have to be, the bound alone decides.
No kernel may reach another device: no remote copies, remote signals or barrier semaphores. Data moves between devices by JAX's collectives and lax.ppermute only.
A program may use at most 64 MiB of HBM per device.

```python
import math
import jax
import jax.numpy as jnp
from jax import lax

BLK = 256
INNER = 8
STEPS = 2
ROWS = 4096
COLS = 8192
N_COL = 16


def draw_matrix(key, part):
    key = jax.random.fold_in(key, 1)
    key_base, key_cols = jax.random.split(key, 2)
    column_scale = jnp.exp(jax.random.uniform(key_cols, (COLS,), jnp.float32, math.log(0.3), math.log(3.0)))
    values = jax.random.truncated_normal(key_base, -4.0, 4.0, (ROWS, COLS), jnp.float32) * column_scale
    return values.astype(jnp.float32)


def place_ends(values, rng, smallest, top_value):
    longest = values.shape.index(max(values.shape))
    spots = []
    for shift in (0, 1):
        where = [jax.random.randint(jax.random.fold_in(rng, axis), (), 0, length) for axis, length in enumerate(values.shape)]
        where[longest] = (where[longest] + shift) % values.shape[longest]
        spots.append(tuple(where))
    return values.at[spots[0]].set(smallest).at[spots[1]].set(top_value)


def setup_inputs(seed: int = 0) -> dict:
    key_list = jax.random.split(jax.random.key(seed), 3)
    return {
        "matrix": draw_matrix(jax.random.fold_in(key_list[2], 71), 0),
        "shifts": place_ends(jax.random.randint(key_list[1], (STEPS, INNER), 0, BLK), jax.random.fold_in(key_list[1], 1), 0, BLK - 1).astype(jnp.int32),
    }


def turn_bottom(gram_blocks, rotation, advance):
    upper_rows = gram_blocks[0]
    lower_rows = jnp.roll(gram_blocks[1], -advance, axis=1)
    stacked = jnp.stack([upper_rows, lower_rows])
    left_cols = stacked[:, 0]
    right_cols = jnp.roll(stacked[:, 1], -advance, axis=2)
    gram_blocks = jnp.stack([left_cols, right_cols], axis=1)
    rotation = jnp.stack([rotation[:, 0], jnp.roll(rotation[:, 1], -advance, axis=1)], axis=1)
    return gram_blocks, rotation


def turn_pairs(gram_blocks, rotation, cosine, sine_part):
    cos_rows = cosine[:, None]
    sin_rows = sine_part[:, None]
    top_left = cos_rows * gram_blocks[0, 0] + sin_rows * gram_blocks[1, 0]
    top_right = cos_rows * gram_blocks[0, 1] + sin_rows * gram_blocks[1, 1]
    low_left = cos_rows * gram_blocks[1, 0] - sin_rows * gram_blocks[0, 0]
    low_right = cos_rows * gram_blocks[1, 1] - sin_rows * gram_blocks[0, 1]
    cos_cols = cosine[None, :]
    sin_cols = sine_part[None, :]
    new_tl = top_left * cos_cols + top_right * sin_cols
    new_tr = top_right * cos_cols - top_left * sin_cols
    new_ll = low_left * cos_cols + low_right * sin_cols
    new_lr = low_right * cos_cols - low_left * sin_cols
    gram_blocks = jnp.stack([jnp.stack([new_tl, new_tr]), jnp.stack([new_ll, new_lr])])
    first_half = rotation[:, 0] * cos_cols + rotation[:, 1] * sin_cols
    second_half = rotation[:, 1] * cos_cols - rotation[:, 0] * sin_cols
    rotation = jnp.stack([first_half, second_half], axis=1)
    return gram_blocks, rotation


def jacobi_pairs(gram_matrix, shift_row):
    block_width = gram_matrix.shape[0] // 2
    gram_blocks = gram_matrix.reshape(2, block_width, 2, block_width).transpose(0, 2, 1, 3)
    rotation = jnp.eye(2 * block_width, dtype=gram_matrix.dtype).reshape(2 * block_width, 2, block_width)
    offset = jnp.zeros((), jnp.int32)
    for inner_index in range(shift_row.shape[0]):
        target = shift_row[inner_index].astype(jnp.int32)
        gram_blocks, rotation = turn_bottom(gram_blocks, rotation, target - offset)
        offset = target
        upper_diag = jnp.diagonal(gram_blocks[0, 0])
        lower_diag = jnp.diagonal(gram_blocks[1, 1])
        coupling = jnp.diagonal(gram_blocks[0, 1])
        angles = 0.5 * jnp.arctan2(2.0 * coupling, upper_diag - lower_diag)
        gram_blocks, rotation = turn_pairs(gram_blocks, rotation, jnp.cos(angles), jnp.sin(angles))
    gram_blocks, rotation = turn_bottom(gram_blocks, rotation, -offset)
    return gram_blocks, rotation.reshape(2 * block_width, 2 * block_width)


def reference(matrix, shifts):
    block_width = BLK
    blocks = matrix.reshape(matrix.shape[0], N_COL, 2 * block_width).transpose(1, 0, 2)
    for section_index in range(STEPS):
        shift_row = shifts[section_index]

        def one_pair(column_pair):
            gram_matrix = jnp.dot(column_pair.T, column_pair, preferred_element_type=jnp.float32, precision=lax.Precision.HIGHEST)
            final_blocks, rotation = jacobi_pairs(gram_matrix, shift_row)
            return jnp.dot(column_pair, rotation, preferred_element_type=jnp.float32, precision=lax.Precision.HIGHEST)

        blocks = lax.map(one_pair, blocks)
        upper_part = jnp.roll(blocks[:, :, :block_width], 1, axis=0)
        lower_part = jnp.roll(blocks[:, :, block_width:], -1, axis=0)
        blocks = jnp.concatenate([upper_part, lower_part], axis=2)
    return blocks.transpose(1, 0, 2).reshape(matrix.shape)
```

```python
import jax
import jax.numpy as jnp
from jax import lax
from jax.experimental import pallas as pl
from jax.experimental.pallas import tpu as pltpu
from jax.sharding import PartitionSpec as P

STEPS = 2


def passed_along(block, axis, distance):
    devices = range(lax.axis_size(axis))
    route = [((i - distance) % len(devices), i) for i in devices]
    return lax.ppermute(block, axis, route)


def half_angle(x, y):
    scale = jnp.maximum(jnp.abs(x), jnp.abs(y))
    flat = scale == 0.0
    inverse = 1.0 / jnp.where(flat, 1.0, scale)
    xs = x * inverse
    ys = y * inverse
    norm = lax.rsqrt(jnp.where(flat, 1.0, xs * xs + ys * ys))
    major = jnp.sqrt(0.5 + 0.5 * jnp.abs(xs * norm))
    minor = 0.5 * jnp.abs(ys * norm) / major
    negative = (y < 0.0) | ((y == 0.0) & (1.0 / y < 0.0))
    ahead = x >= 0.0
    cosine = jnp.where(flat, 1.0, jnp.where(ahead, major, minor))
    sine = jnp.where(ahead, minor, major)
    sine = jnp.where(negative, -sine, sine)
    return cosine, jnp.where(flat, 0.0, sine)


def inner_kernel(shift_ref, gram_ref, pair_ref, out_ref, tl, tr, lr):
    w = tl.shape[0]
    tl[...] = gram_ref[:w, :w]
    tr[...] = gram_ref[:w, w:]
    lr[...] = gram_ref[w:, w:]
    out_ref[...] = pair_ref[...]
    rows = lax.broadcasted_iota(jnp.int32, (w, w), 0)
    cols = lax.broadcasted_iota(jnp.int32, (w, w), 1)
    eye = rows == cols

    def diagonal(block):
        return jnp.sum(jnp.where(eye, block, 0.0), axis=0, keepdims=True)

    def as_rows(vector):
        half = jnp.transpose(jnp.broadcast_to(vector, (w // 2, w)))
        return jnp.concatenate([half, half], axis=1)

    def one_round(r, offset):
        target = shift_ref[r]
        back = lax.rem(offset - target + 2 * w, w)
        top_left = tl[...]
        top_right = pltpu.roll(tr[...], back, 1)
        low_right = pltpu.roll(pltpu.roll(lr[...], back, 1), back, 0)
        c, s = half_angle(
            diagonal(top_left) - diagonal(low_right), 2.0 * diagonal(top_right)
        )
        c_rows = as_rows(c)
        s_rows = as_rows(s)
        low_left = jnp.transpose(top_right)
        half_tl = c_rows * top_left + s_rows * low_left
        half_tr = c_rows * top_right + s_rows * low_right
        half_ll = c_rows * low_left - s_rows * top_left
        half_lr = c_rows * low_right - s_rows * top_right
        tl[...] = half_tl * c + half_tr * s
        tr[...] = half_tr * c - half_tl * s
        lr[...] = half_lr * c - half_ll * s
        upper = out_ref[:, :w]
        lower = pltpu.roll(out_ref[:, w:], back, 1)
        out_ref[:, :w] = upper * c + lower * s
        out_ref[:, w:] = lower * c - upper * s
        return target

    last = lax.fori_loop(0, shift_ref.shape[0], one_round, jnp.int32(0))
    out_ref[:, w:] = pltpu.roll(out_ref[:, w:], last, 1)


def rotated_pair(shift_row, gram_matrix, column_pair):
    w = column_pair.shape[1] // 2
    return pl.pallas_call(
        inner_kernel,
        out_shape=jax.ShapeDtypeStruct(column_pair.shape, jnp.float32),
        in_specs=[
            pl.BlockSpec(memory_space=pltpu.SMEM),
            pl.BlockSpec(memory_space=pltpu.VMEM),
            pl.BlockSpec(memory_space=pltpu.VMEM),
        ],
        out_specs=pl.BlockSpec(memory_space=pltpu.VMEM),
        scratch_shapes=[pltpu.VMEM((w, w), jnp.float32)] * 3,
        compiler_params=pltpu.CompilerParams(vmem_limit_bytes=32 * 1024 * 1024),
    )(shift_row, gram_matrix, column_pair)


def local_gram(left_part, right_part):
    return lax.dot_general(
        left_part,
        right_part,
        (((0,), (0,)), ((), ())),
        precision=lax.Precision.HIGHEST,
        preferred_element_type=jnp.float32,
    )


def whole_gram(column_pair):
    return lax.psum(local_gram(column_pair, column_pair), "row")


def trade_blocks(upper_rows, lower_rows):
    upper_rows = passed_along(upper_rows, "col", 1)
    lower_rows = passed_along(lower_rows, "col", -1)
    return (upper_rows, lower_rows)


def per_device(matrix, shifts):
    block_width = matrix.shape[1] // 2
    column_pair = matrix
    for section_index in range(STEPS):
        gram_matrix = whole_gram(column_pair)
        column_pair = rotated_pair(shifts[section_index], gram_matrix, column_pair)
        upper_rows, lower_rows = trade_blocks(
            column_pair[:, :block_width], column_pair[:, block_width:]
        )
        column_pair = jnp.concatenate([upper_rows, lower_rows], axis=1)
    return column_pair


def solution(mesh):
    in_specs = (P("row", "col"), P())
    out_specs = P("row", "col")
    return jax.shard_map(
        per_device, mesh=mesh, in_specs=in_specs, out_specs=out_specs, check_vma=False
    )
```

```python
import jax
import jax.numpy as jnp
from jax import lax
from jax.experimental import pallas as pl
from jax.experimental.pallas import tpu as pltpu
from jax.sharding import PartitionSpec as P

LANES = 128
VMEM = pl.BlockSpec(memory_space=pltpu.VMEM)
SMEM = pl.BlockSpec(memory_space=pltpu.SMEM)


def kernel_call(kernel, outs, ins, scratch=()):
    return pl.pallas_call(
        kernel,
        out_shape=[jax.ShapeDtypeStruct(shape, jnp.float32) for shape in outs],
        in_specs=ins,
        out_specs=[VMEM] * len(outs),
        scratch_shapes=[pltpu.VMEM(shape, jnp.float32) for shape in scratch],
        compiler_params=pltpu.CompilerParams(vmem_limit_bytes=32 * 1024 * 1024),
    )


def half_angle(x, y):
    scale = jnp.maximum(jnp.abs(x), jnp.abs(y))
    flat = scale == 0.0
    inverse = 1.0 / jnp.where(flat, 1.0, scale)
    xs = x * inverse
    ys = y * inverse
    norm = lax.rsqrt(jnp.where(flat, 1.0, xs * xs + ys * ys))
    major = jnp.sqrt(0.5 + 0.5 * jnp.abs(xs * norm))
    minor = 0.5 * jnp.abs(ys * norm) / major
    negative = (y < 0.0) | ((y == 0.0) & (1.0 / y < 0.0))
    ahead = x >= 0.0
    cosine = jnp.where(flat, 1.0, jnp.where(ahead, major, minor))
    sine = jnp.where(ahead, minor, major)
    sine = jnp.where(negative, -sine, sine)
    return cosine, jnp.where(flat, 0.0, sine)


def grid_of(w):
    rows = lax.broadcasted_iota(jnp.int32, (w, w), 0)
    cols = lax.broadcasted_iota(jnp.int32, (w, w), 1)
    return rows, cols


def diagonal(block):
    rows, cols = grid_of(block.shape[0])
    return jnp.sum(jnp.where(rows == cols, block, 0.0), axis=0, keepdims=True)


def inner_rounds(shift_ref, tl, tr, lr, upper_ref, lower_ref):
    w = tl.shape[0]

    def as_rows(vector):
        half = jnp.transpose(jnp.broadcast_to(vector, (LANES, w)))
        return jnp.concatenate([half] * (w // LANES), axis=1)

    def one_round(r, offset):
        target = shift_ref[r]
        back = lax.rem(offset - target + 2 * w, w)
        top_left = tl[...]
        top_right = pltpu.roll(tr[...], back, 1)
        low_right = pltpu.roll(pltpu.roll(lr[...], back, 1), back, 0)
        c, s = half_angle(
            diagonal(top_left) - diagonal(low_right), 2.0 * diagonal(top_right)
        )
        c_rows = as_rows(c)
        s_rows = as_rows(s)
        low_left = jnp.transpose(top_right)
        half_tl = c_rows * top_left + s_rows * low_left
        half_tr = c_rows * top_right + s_rows * low_right
        half_ll = c_rows * low_left - s_rows * top_left
        half_lr = c_rows * low_right - s_rows * top_right
        tl[...] = half_tl * c + half_tr * s
        tr[...] = half_tr * c - half_tl * s
        lr[...] = half_lr * c - half_ll * s
        upper = upper_ref[...]
        lower = pltpu.roll(lower_ref[...], back, 1)
        upper_ref[...] = upper * c + lower * s
        lower_ref[...] = lower * c - upper * s
        return target

    last = lax.fori_loop(0, shift_ref.shape[0], one_round, jnp.int32(0))
    lower_ref[...] = pltpu.roll(lower_ref[...], last, 1)
    lr[...] = pltpu.roll(pltpu.roll(lr[...], last, 1), last, 0)


def full_dot(left, right):
    return lax.dot_general(
        left,
        right,
        (((0,), (0,)), ((), ())),
        precision=lax.Precision.HIGHEST,
        preferred_element_type=jnp.float32,
    )


def write_pieces(out_ref, block, start):
    pieces = out_ref.shape[0]
    share = block.shape[0] // pieces
    for p in range(pieces):
        for t in range(block.shape[1] // LANES):
            out_ref[p, start + t * share : start + (t + 1) * share, :] = block[
                p * share : (p + 1) * share, t * LANES : (t + 1) * LANES
            ]


def read_pieces(in_ref, out_ref, start):
    pieces = in_ref.shape[0]
    share = out_ref.shape[0] // pieces
    for p in range(pieces):
        for t in range(out_ref.shape[1] // LANES):
            out_ref[p * share : (p + 1) * share, t * LANES : (t + 1) * LANES] = in_ref[
                p, start + t * share : start + (t + 1) * share, :
            ]


def gram_kernel(pair_ref, out_ref):
    w = pair_ref.shape[1] // 2
    rows, cols = grid_of(w)
    upper = pair_ref[:, :w]
    lower = pair_ref[:, w:]
    low_right = full_dot(lower, lower)
    write_pieces(out_ref, jnp.where(rows <= cols, full_dot(upper, upper), low_right), 0)
    write_pieces(out_ref, full_dot(upper, lower), 2 * w * w // (out_ref.shape[0] * 2 * LANES))
    low_diag = diagonal(low_right)
    end = out_ref.shape[1] - 8
    for p in range(out_ref.shape[0]):
        out_ref[p, end:, :] = jnp.zeros((8, LANES), jnp.float32)
        for t in range(w // LANES):
            out_ref[p, end + t : end + t + 1, :] = low_diag[:, t * LANES : (t + 1) * LANES]


def cross_kernel(upper_ref, lower_ref, out_ref):
    write_pieces(out_ref, full_dot(upper_ref[...], lower_ref[...]), 0)


def first_kernel(shift_ref, gram_ref, pair_ref, upper_ref, lower_ref, tl, lr, tr):
    w = tl.shape[0]
    rows, cols = grid_of(w)
    read_pieces(gram_ref, tl, 0)
    read_pieces(gram_ref, tr, w * w // (gram_ref.shape[0] * LANES))
    square = tl[...]
    turned = jnp.transpose(square)
    end = gram_ref.shape[1] - 8
    low_diag = jnp.concatenate(
        [gram_ref[0, end + t : end + t + 1, :] for t in range(w // LANES)], axis=1
    )
    lr[...] = jnp.where(rows == cols, low_diag, jnp.where(rows > cols, square, turned))
    tl[...] = jnp.where(rows <= cols, square, turned)
    upper_ref[...] = pair_ref[:, :w]
    lower_ref[...] = pair_ref[:, w:]
    inner_rounds(shift_ref, tl, tr, lr, upper_ref, lower_ref)


def second_kernel(
    shift_ref, tl_ref, cross_ref, lr_ref, upper_in, lower_in, upper_ref, lower_ref, tl, tr, lr
):
    tl[...] = tl_ref[...]
    lr[...] = lr_ref[...]
    read_pieces(cross_ref, tr, 0)
    upper_ref[...] = upper_in[...]
    lower_ref[...] = lower_in[...]
    inner_rounds(shift_ref, tl, tr, lr, upper_ref, lower_ref)


def passed_along(block, axis, distance):
    devices = range(lax.axis_size(axis))
    route = [((i - distance) % len(devices), i) for i in devices]
    return lax.ppermute(block, axis, route)


def summed_pieces(pieces, axis):
    mine = lax.all_to_all(pieces, axis, 0, 0, tiled=True).sum(0, keepdims=True)
    return lax.all_to_all(jnp.broadcast_to(mine, pieces.shape), axis, 0, 0, tiled=True)


def per_device(matrix, shifts):
    rows, width = matrix.shape
    w = width // 2
    n = lax.axis_size("row")
    block = (rows, w)
    square = (w, w)
    share = w * w // (n * LANES)

    (pieces,) = kernel_call(gram_kernel, [(n, 2 * share + 8, LANES)], [VMEM])(matrix)
    upper, lower, tl, lr = kernel_call(
        first_kernel, [block, block, square, square], [SMEM, VMEM, VMEM], [square]
    )(shifts[0], summed_pieces(pieces, "row"), matrix)
    upper = passed_along(upper, "col", 1)
    lower = passed_along(lower, "col", -1)
    tl = passed_along(tl, "col", 1)
    lr = passed_along(lr, "col", -1)

    (pieces,) = kernel_call(cross_kernel, [(n, share, LANES)], [VMEM, VMEM])(upper, lower)
    upper, lower = kernel_call(
        second_kernel, [block, block], [SMEM] + [VMEM] * 5, [square] * 3
    )(shifts[1], tl, summed_pieces(pieces, "row"), lr, upper, lower)
    upper = passed_along(upper, "col", 1)
    lower = passed_along(lower, "col", -1)
    return jnp.concatenate([upper, lower], axis=1)


def solution(mesh):
    in_specs = (P("row", "col"), P())
    out_specs = P("row", "col")
    return jax.shard_map(
        per_device, mesh=mesh, in_specs=in_specs, out_specs=out_specs, check_vma=False
    )
```

```python
import jax
import jax.numpy as jnp
from jax import lax
from jax.experimental import pallas as pl
from jax.experimental.pallas import tpu as pltpu
from jax.sharding import PartitionSpec as P

LANES = 128
VMEM = pl.BlockSpec(memory_space=pltpu.VMEM)
SMEM = pl.BlockSpec(memory_space=pltpu.SMEM)


def kernel_call(kernel, outs, ins, scratch=()):
    return pl.pallas_call(
        kernel,
        out_shape=[jax.ShapeDtypeStruct(shape, jnp.float32) for shape in outs],
        in_specs=ins,
        out_specs=[VMEM] * len(outs),
        scratch_shapes=[pltpu.VMEM(shape, jnp.float32) for shape in scratch],
        compiler_params=pltpu.CompilerParams(vmem_limit_bytes=32 * 1024 * 1024),
    )


def half_angle(x, y):
    scale = jnp.maximum(jnp.abs(x), jnp.abs(y))
    flat = scale == 0.0
    inverse = 1.0 / jnp.where(flat, 1.0, scale)
    xs = x * inverse
    ys = y * inverse
    norm = lax.rsqrt(jnp.where(flat, 1.0, xs * xs + ys * ys))
    major = jnp.sqrt(0.5 + 0.5 * jnp.abs(xs * norm))
    minor = 0.5 * jnp.abs(ys * norm) / major
    negative = (y < 0.0) | ((y == 0.0) & (1.0 / y < 0.0))
    ahead = x >= 0.0
    cosine = jnp.where(flat, 1.0, jnp.where(ahead, major, minor))
    sine = jnp.where(ahead, minor, major)
    sine = jnp.where(negative, -sine, sine)
    return cosine, jnp.where(flat, 0.0, sine)


def grid_of(w):
    rows = lax.broadcasted_iota(jnp.int32, (w, w), 0)
    cols = lax.broadcasted_iota(jnp.int32, (w, w), 1)
    return rows, cols


def diagonal(block):
    rows, cols = grid_of(block.shape[0])
    return jnp.sum(jnp.where(rows == cols, block, 0.0), axis=0, keepdims=True)


def inner_rounds(shift_ref, tl, tr, lr, upper_ref, lower_ref):
    w = tl.shape[0]

    def as_rows(vector):
        half = jnp.transpose(jnp.broadcast_to(vector, (LANES, w)))
        return jnp.concatenate([half] * (w // LANES), axis=1)

    def one_round(r, offset):
        target = shift_ref[r]
        back = lax.rem(offset - target + 2 * w, w)
        top_left = tl[...]
        top_right = pltpu.roll(tr[...], back, 1)
        low_right = pltpu.roll(pltpu.roll(lr[...], back, 1), back, 0)
        c, s = half_angle(
            diagonal(top_left) - diagonal(low_right), 2.0 * diagonal(top_right)
        )
        c_rows = as_rows(c)
        s_rows = as_rows(s)
        low_left = jnp.transpose(top_right)
        half_tl = c_rows * top_left + s_rows * low_left
        half_tr = c_rows * top_right + s_rows * low_right
        half_ll = c_rows * low_left - s_rows * top_left
        half_lr = c_rows * low_right - s_rows * top_right
        tl[...] = half_tl * c + half_tr * s
        tr[...] = half_tr * c - half_tl * s
        lr[...] = half_lr * c - half_ll * s
        upper = upper_ref[...]
        lower = pltpu.roll(lower_ref[...], back, 1)
        upper_ref[...] = upper * c + lower * s
        lower_ref[...] = lower * c - upper * s
        return target

    last = lax.fori_loop(0, shift_ref.shape[0], one_round, jnp.int32(0))
    lower_ref[...] = pltpu.roll(lower_ref[...], last, 1)
    lr[...] = pltpu.roll(pltpu.roll(lr[...], last, 1), last, 0)


def full_dot(left, right):
    return lax.dot_general(
        left,
        right,
        (((0,), (0,)), ((), ())),
        precision=lax.Precision.HIGHEST,
        preferred_element_type=jnp.float32,
    )


def hand_out(place_ref, blocks, outs):
    for k, out in enumerate(outs):
        start = 0
        for block in blocks:
            share = block.shape[0] // len(outs)
            quarter = (place_ref[0] ^ k) * share
            out[start : start + share, :] = block[pl.ds(pl.multiple_of(quarter, 8), share), :]
            start += share


def take_in(place_ref, ins, blocks):
    for k, piece in enumerate(ins):
        start = 0
        for block in blocks:
            share = block.shape[0] // len(ins)
            quarter = (place_ref[0] ^ k) * share
            block[pl.ds(pl.multiple_of(quarter, 8), share), :] = piece[start : start + share, :]
            start += share


def gram_kernel(place_ref, pair_ref, out0, out1, out2, out3, square, cross, diag):
    outs = (out0, out1, out2, out3)
    w = pair_ref.shape[1] // 2
    rows, cols = grid_of(w)
    upper = pair_ref[:, :w]
    lower = pair_ref[:, w:]
    low_right = full_dot(lower, lower)
    square[...] = jnp.where(rows <= cols, full_dot(upper, upper), low_right)
    cross[...] = full_dot(upper, lower)
    diag[...] = jnp.broadcast_to(diagonal(low_right), diag.shape)
    hand_out(place_ref, (square, cross, diag), outs)


def cross_kernel(place_ref, upper_ref, lower_ref, out0, out1, out2, out3, cross):
    cross[...] = full_dot(upper_ref[...], lower_ref[...])
    hand_out(place_ref, (cross,), (out0, out1, out2, out3))


def first_kernel(
    place_ref, shift_ref, in0, in1, in2, in3, pair_ref, upper_ref, lower_ref, tl, lr, tr, diag
):
    w = tl.shape[0]
    rows, cols = grid_of(w)
    take_in(place_ref, (in0, in1, in2, in3), (tl, tr, diag))
    square = tl[...]
    turned = jnp.transpose(square)
    lr[...] = jnp.where(rows == cols, diag[:1, :], jnp.where(rows > cols, square, turned))
    tl[...] = jnp.where(rows <= cols, square, turned)
    upper_ref[...] = pair_ref[:, :w]
    lower_ref[...] = pair_ref[:, w:]
    inner_rounds(shift_ref, tl, tr, lr, upper_ref, lower_ref)


def second_kernel(
    place_ref,
    shift_ref,
    in0,
    in1,
    in2,
    in3,
    tl_ref,
    lr_ref,
    upper_in,
    lower_in,
    upper_ref,
    lower_ref,
    tl,
    tr,
    lr,
):
    tl[...] = tl_ref[...]
    lr[...] = lr_ref[...]
    take_in(place_ref, (in0, in1, in2, in3), (tr,))
    upper_ref[...] = upper_in[...]
    lower_ref[...] = lower_in[...]
    inner_rounds(shift_ref, tl, tr, lr, upper_ref, lower_ref)


def passed_along(block, axis, distance):
    devices = range(lax.axis_size(axis))
    route = [((i - distance) % len(devices), i) for i in devices]
    return lax.ppermute(block, axis, route)


def swapped(block, axis, bits):
    return lax.ppermute(block, axis, [(i, i ^ bits) for i in range(lax.axis_size(axis))])


def summed_quarters(outs, axis):
    sent = [swapped(outs[k], axis, k) for k in (3, 1, 2)]
    mine = (outs[0] + sent[1]) + (sent[2] + sent[0])
    met = [swapped(mine, axis, k) for k in (8, 4, 12)]
    mine = (mine + met[1]) + (met[0] + met[2])
    shared = [swapped(mine, axis, k) for k in (3, 1, 2)]
    return (mine, shared[1], shared[2], shared[0])


def per_device(matrix, shifts):
    rows, width = matrix.shape
    w = width // 2
    block = (rows, w)
    square = (w, w)
    diag = (32, w)
    place = (lax.axis_index("row") % 4).astype(jnp.int32).reshape(1)

    quarters = kernel_call(
        gram_kernel, [(2 * w // 4 + 8, w)] * 4, [SMEM, VMEM], [square, square, diag]
    )(place, matrix)
    upper, lower, tl, lr = kernel_call(
        first_kernel, [block, block, square, square], [SMEM, SMEM] + [VMEM] * 5, [square, diag]
    )(place, shifts[0], *summed_quarters(quarters, "row"), matrix)
    upper = passed_along(upper, "col", 1)
    lower = passed_along(lower, "col", -1)
    tl = passed_along(tl, "col", 1)
    lr = passed_along(lr, "col", -1)

    quarters = kernel_call(
        cross_kernel, [(w // 4, w)] * 4, [SMEM, VMEM, VMEM], [square]
    )(place, upper, lower)
    upper, lower = kernel_call(
        second_kernel, [block, block], [SMEM, SMEM] + [VMEM] * 8, [square] * 3
    )(place, shifts[1], *summed_quarters(quarters, "row"), tl, lr, upper, lower)
    upper = passed_along(upper, "col", 1)
    lower = passed_along(lower, "col", -1)
    return jnp.concatenate([upper, lower], axis=1)


def solution(mesh):
    in_specs = (P("row", "col"), P())
    out_specs = P("row", "col")
    return jax.shard_map(
        per_device, mesh=mesh, in_specs=in_specs, out_specs=out_specs, check_vma=False
    )
```

```python
import jax
import jax.numpy as jnp
from jax import lax
from jax.experimental import pallas as pl
from jax.experimental.pallas import tpu as pltpu
from jax.sharding import PartitionSpec as P

LANES = 128
VMEM = pl.BlockSpec(memory_space=pltpu.VMEM)
SMEM = pl.BlockSpec(memory_space=pltpu.SMEM)


def kernel_call(kernel, outs, ins, scratch=()):
    return pl.pallas_call(
        kernel,
        out_shape=[jax.ShapeDtypeStruct(shape, jnp.float32) for shape in outs],
        in_specs=ins,
        out_specs=[VMEM] * len(outs),
        scratch_shapes=[pltpu.VMEM(shape, jnp.float32) for shape in scratch],
        compiler_params=pltpu.CompilerParams(vmem_limit_bytes=32 * 1024 * 1024),
    )


def half_angle(x, y):
    scale = jnp.maximum(jnp.abs(x), jnp.abs(y))
    flat = scale == 0.0
    inverse = 1.0 / jnp.where(flat, 1.0, scale)
    xs = x * inverse
    ys = y * inverse
    norm = lax.rsqrt(jnp.where(flat, 1.0, xs * xs + ys * ys))
    major = jnp.sqrt(0.5 + 0.5 * jnp.abs(xs * norm))
    minor = 0.5 * jnp.abs(ys * norm) / major
    negative = (y < 0.0) | ((y == 0.0) & (1.0 / y < 0.0))
    ahead = x >= 0.0
    cosine = jnp.where(flat, 1.0, jnp.where(ahead, major, minor))
    sine = jnp.where(ahead, minor, major)
    sine = jnp.where(negative, -sine, sine)
    return cosine, jnp.where(flat, 0.0, sine)


def grid_of(w):
    rows = lax.broadcasted_iota(jnp.int32, (w, w), 0)
    cols = lax.broadcasted_iota(jnp.int32, (w, w), 1)
    return rows, cols


def diagonal(block):
    rows, cols = grid_of(LANES)
    parts = [
        jnp.sum(jnp.where(rows == cols, block[t : t + LANES, t : t + LANES], 0.0), 0, keepdims=True)
        for t in range(0, block.shape[0], LANES)
    ]
    return jnp.concatenate(parts, axis=1)


def turned_along(vector, back):
    return pltpu.roll(jnp.broadcast_to(vector, (8, vector.shape[1])), back, 1)[:1]


def inner_rounds(shift_ref, tl, tr, lr, upper_ref, lower_ref):
    w = tl.shape[0]

    def as_rows(vector):
        half = jnp.transpose(jnp.broadcast_to(vector, (LANES, w)))
        return jnp.concatenate([half] * (w // LANES), axis=1)

    offset = jnp.int32(0)
    a = diagonal(tl[...])
    b = diagonal(lr[...])
    for r in range(shift_ref.shape[0]):
        target = shift_ref[r]
        back = lax.rem(offset - target + 2 * w, w)
        offset = target
        top_left = tl[...]
        top_right = pltpu.roll(tr[...], back, 1)
        low_right = pltpu.roll(pltpu.roll(lr[...], back, 1), back, 0)
        g = diagonal(top_right)
        b = turned_along(b, back)
        c, s = half_angle(a - b, 2.0 * g)
        a, b = (
            (c * a + s * g) * c + (c * g + s * b) * s,
            (c * b - s * g) * c - (c * g - s * a) * s,
        )
        c_rows = as_rows(c)
        s_rows = as_rows(s)
        low_left = jnp.transpose(top_right)
        half_tl = c_rows * top_left + s_rows * low_left
        half_tr = c_rows * top_right + s_rows * low_right
        half_ll = c_rows * low_left - s_rows * top_left
        half_lr = c_rows * low_right - s_rows * top_right
        tl[...] = half_tl * c + half_tr * s
        tr[...] = half_tr * c - half_tl * s
        lr[...] = half_lr * c - half_ll * s
        upper = upper_ref[...]
        lower = pltpu.roll(lower_ref[...], back, 1)
        upper_ref[...] = upper * c + lower * s
        lower_ref[...] = lower * c - upper * s
    lower_ref[...] = pltpu.roll(lower_ref[...], offset, 1)
    lr[...] = pltpu.roll(pltpu.roll(lr[...], offset, 1), offset, 0)


def full_dot(left, right):
    return lax.dot_general(
        left,
        right,
        (((0,), (0,)), ((), ())),
        precision=lax.Precision.HIGHEST,
        preferred_element_type=jnp.float32,
    )


def hand_out(place_ref, blocks, outs):
    for k, out in enumerate(outs):
        start = 0
        for block in blocks:
            share = block.shape[0] // len(outs)
            quarter = (place_ref[0] ^ k) * share
            out[start : start + share, :] = block[pl.ds(pl.multiple_of(quarter, 8), share), :]
            start += share


def take_in(place_ref, ins, blocks):
    for k, piece in enumerate(ins):
        start = 0
        for block in blocks:
            share = block.shape[0] // len(ins)
            quarter = (place_ref[0] ^ k) * share
            block[pl.ds(pl.multiple_of(quarter, 8), share), :] = piece[start : start + share, :]
            start += share


def gram_kernel(place_ref, pair_ref, out0, out1, out2, out3, square, cross, diag):
    outs = (out0, out1, out2, out3)
    w = pair_ref.shape[1] // 2
    rows, cols = grid_of(w)
    upper = pair_ref[:, :w]
    lower = pair_ref[:, w:]
    low_right = full_dot(lower, lower)
    square[...] = jnp.where(rows <= cols, full_dot(upper, upper), low_right)
    cross[...] = full_dot(upper, lower)
    diag[...] = jnp.broadcast_to(diagonal(low_right), diag.shape)
    hand_out(place_ref, (square, cross, diag), outs)


def cross_kernel(place_ref, upper_ref, lower_ref, out0, out1, out2, out3, cross):
    cross[...] = full_dot(upper_ref[...], lower_ref[...])
    hand_out(place_ref, (cross,), (out0, out1, out2, out3))


def first_kernel(
    place_ref, shift_ref, in0, in1, in2, in3, pair_ref, upper_ref, lower_ref, tl, lr, tr, diag
):
    w = tl.shape[0]
    rows, cols = grid_of(w)
    take_in(place_ref, (in0, in1, in2, in3), (tl, tr, diag))
    square = tl[...]
    turned = jnp.transpose(square)
    lr[...] = jnp.where(rows == cols, diag[:1, :], jnp.where(rows > cols, square, turned))
    tl[...] = jnp.where(rows <= cols, square, turned)
    upper_ref[...] = pair_ref[:, :w]
    lower_ref[...] = pair_ref[:, w:]
    inner_rounds(shift_ref, tl, tr, lr, upper_ref, lower_ref)


def second_kernel(
    place_ref,
    shift_ref,
    in0,
    in1,
    in2,
    in3,
    tl_ref,
    lr_ref,
    upper_in,
    lower_in,
    upper_ref,
    lower_ref,
    tl,
    tr,
    lr,
):
    tl[...] = tl_ref[...]
    lr[...] = lr_ref[...]
    take_in(place_ref, (in0, in1, in2, in3), (tr,))
    upper_ref[...] = upper_in[...]
    lower_ref[...] = lower_in[...]
    inner_rounds(shift_ref, tl, tr, lr, upper_ref, lower_ref)


def passed_along(block, axis, distance):
    devices = range(lax.axis_size(axis))
    route = [((i - distance) % len(devices), i) for i in devices]
    return lax.ppermute(block, axis, route)


def swapped(block, axis, bits):
    return lax.ppermute(block, axis, [(i, i ^ bits) for i in range(lax.axis_size(axis))])


def summed_quarters(outs, axis):
    sent = [swapped(outs[k], axis, k) for k in (3, 1, 2)]
    mine = (outs[0] + sent[1]) + (sent[2] + sent[0])
    met = [swapped(mine, axis, k) for k in (8, 4, 12)]
    mine = (mine + met[1]) + (met[0] + met[2])
    shared = [swapped(mine, axis, k) for k in (3, 1, 2)]
    return (mine, shared[1], shared[2], shared[0])


def per_device(matrix, shifts):
    rows, width = matrix.shape
    w = width // 2
    block = (rows, w)
    square = (w, w)
    diag = (32, w)
    place = (lax.axis_index("row") % 4).astype(jnp.int32).reshape(1)

    quarters = kernel_call(
        gram_kernel, [(2 * w // 4 + 8, w)] * 4, [SMEM, VMEM], [square, square, diag]
    )(place, matrix)
    upper, lower, tl, lr = kernel_call(
        first_kernel, [block, block, square, square], [SMEM, SMEM] + [VMEM] * 5, [square, diag]
    )(place, shifts[0], *summed_quarters(quarters, "row"), matrix)
    upper = passed_along(upper, "col", 2)
    tl = passed_along(tl, "col", 2)

    quarters = kernel_call(
        cross_kernel, [(w // 4, w)] * 4, [SMEM, VMEM, VMEM], [square]
    )(place, upper, lower)
    upper, lower = kernel_call(
        second_kernel, [block, block], [SMEM, SMEM] + [VMEM] * 8, [square] * 3
    )(place, shifts[1], *summed_quarters(quarters, "row"), tl, lr, upper, lower)
    lower = passed_along(lower, "col", -2)
    return jnp.concatenate([upper, lower], axis=1)


def solution(mesh):
    in_specs = (P("row", "col"), P())
    out_specs = P("row", "col")
    return jax.shard_map(
        per_device, mesh=mesh, in_specs=in_specs, out_specs=out_specs, check_vma=False
    )
```

```python
import jax
import jax.numpy as jnp
from jax import lax
from jax.experimental import pallas as pl
from jax.experimental.pallas import tpu as pltpu
from jax.sharding import PartitionSpec as P

LANES = 128
VMEM = pl.BlockSpec(memory_space=pltpu.VMEM)
SMEM = pl.BlockSpec(memory_space=pltpu.SMEM)


def kernel_call(kernel, outs, ins, scratch=()):
    return pl.pallas_call(
        kernel,
        out_shape=[jax.ShapeDtypeStruct(shape, jnp.float32) for shape in outs],
        in_specs=ins,
        out_specs=[VMEM] * len(outs),
        scratch_shapes=[pltpu.VMEM(shape, jnp.float32) for shape in scratch],
        compiler_params=pltpu.CompilerParams(vmem_limit_bytes=32 * 1024 * 1024),
    )


def half_angle(x, y):
    scale = jnp.maximum(jnp.abs(x), jnp.abs(y))
    flat = scale == 0.0
    inverse = 1.0 / jnp.where(flat, 1.0, scale)
    xs = x * inverse
    ys = y * inverse
    norm = lax.rsqrt(jnp.where(flat, 1.0, xs * xs + ys * ys))
    major = jnp.sqrt(0.5 + 0.5 * jnp.abs(xs * norm))
    minor = 0.5 * jnp.abs(ys * norm) / major
    negative = (y < 0.0) | ((y == 0.0) & (1.0 / y < 0.0))
    ahead = x >= 0.0
    cosine = jnp.where(flat, 1.0, jnp.where(ahead, major, minor))
    sine = jnp.where(ahead, minor, major)
    sine = jnp.where(negative, -sine, sine)
    return cosine, jnp.where(flat, 0.0, sine)


def grid_of(w):
    rows = lax.broadcasted_iota(jnp.int32, (w, w), 0)
    cols = lax.broadcasted_iota(jnp.int32, (w, w), 1)
    return rows, cols


def diagonal(block):
    rows, cols = grid_of(LANES)
    parts = [
        jnp.sum(jnp.where(rows == cols, block[t : t + LANES, t : t + LANES], 0.0), 0, keepdims=True)
        for t in range(0, block.shape[0], LANES)
    ]
    return jnp.concatenate(parts, axis=1)


def turned_along(vector, back):
    return pltpu.roll(jnp.broadcast_to(vector, (8, vector.shape[1])), back, 1)[:1]


def inner_rounds(shift_ref, tl, tr, lr, upper_ref, lower_ref, angles_ref=None):
    w = tl.shape[0]

    def as_rows(vector):
        half = jnp.transpose(jnp.broadcast_to(vector, (LANES, w)))
        return jnp.concatenate([half] * (w // LANES), axis=1)

    offset = jnp.int32(0)
    a = diagonal(tl[...])
    b = diagonal(lr[...])
    for r in range(shift_ref.shape[0]):
        target = shift_ref[r]
        back = lax.rem(offset - target + 2 * w, w)
        offset = target
        top_left = tl[...]
        top_right = pltpu.roll(tr[...], back, 1)
        low_right = pltpu.roll(pltpu.roll(lr[...], back, 1), back, 0)
        g = diagonal(top_right)
        b = turned_along(b, back)
        c, s = half_angle(a - b, 2.0 * g)
        a, b = (
            (c * a + s * g) * c + (c * g + s * b) * s,
            (c * b - s * g) * c - (c * g - s * a) * s,
        )
        if angles_ref is not None:
            angles_ref[2 * r : 2 * r + 1, :] = c
            angles_ref[2 * r + 1 : 2 * r + 2, :] = s
        c_rows = as_rows(c)
        s_rows = as_rows(s)
        low_left = jnp.transpose(top_right)
        half_tl = c_rows * top_left + s_rows * low_left
        half_tr = c_rows * top_right + s_rows * low_right
        half_ll = c_rows * low_left - s_rows * top_left
        half_lr = c_rows * low_right - s_rows * top_right
        tl[...] = half_tl * c + half_tr * s
        tr[...] = half_tr * c - half_tl * s
        lr[...] = half_lr * c - half_ll * s
        upper = upper_ref[...]
        lower = pltpu.roll(lower_ref[...], back, 1)
        upper_ref[...] = upper * c + lower * s
        lower_ref[...] = lower * c - upper * s
    lower_ref[...] = pltpu.roll(lower_ref[...], offset, 1)
    lr[...] = pltpu.roll(pltpu.roll(lr[...], offset, 1), offset, 0)


def replayed_rounds(shift_ref, angles_ref, left, right):
    w = left.shape[1]
    offset = jnp.int32(0)
    for r in range(shift_ref.shape[0]):
        target = shift_ref[r]
        back = lax.rem(offset - target + 2 * w, w)
        offset = target
        c = angles_ref[2 * r : 2 * r + 1, :]
        s = angles_ref[2 * r + 1 : 2 * r + 2, :]
        upper = left[...]
        lower = pltpu.roll(right[...], back, 1)
        left[...] = upper * c + lower * s
        right[...] = lower * c - upper * s
    right[...] = pltpu.roll(right[...], offset, 1)


def full_dot(left, right):
    return lax.dot_general(
        left,
        right,
        (((0,), (0,)), ((), ())),
        precision=lax.Precision.HIGHEST,
        preferred_element_type=jnp.float32,
    )


def hand_out(place_ref, blocks, outs):
    for k, out in enumerate(outs):
        start = 0
        for block in blocks:
            share = block.shape[0] // len(outs)
            quarter = (place_ref[0] ^ k) * share
            out[start : start + share, :] = block[pl.ds(pl.multiple_of(quarter, 8), share), :]
            start += share


def take_in(place_ref, ins, blocks):
    for k, piece in enumerate(ins):
        start = 0
        for block in blocks:
            share = block.shape[0] // len(ins)
            quarter = (place_ref[0] ^ k) * share
            block[pl.ds(pl.multiple_of(quarter, 8), share), :] = piece[start : start + share, :]
            start += share


def gram_kernel(place_ref, pair_ref, out0, out1, out2, out3, square, cross, diag):
    outs = (out0, out1, out2, out3)
    w = pair_ref.shape[1] // 2
    rows, cols = grid_of(w)
    upper = pair_ref[:, :w]
    lower = pair_ref[:, w:]
    low_right = full_dot(lower, lower)
    square[...] = jnp.where(rows <= cols, full_dot(upper, upper), low_right)
    cross[...] = full_dot(upper, lower)
    diag[...] = jnp.broadcast_to(diagonal(low_right), diag.shape)
    hand_out(place_ref, (square, cross, diag), outs)


def cross_kernel(place_ref, left_ref, right_ref, out0, out1, out2, out3, cross):
    cross[...] = full_dot(left_ref[...], right_ref[...])
    hand_out(place_ref, (cross,), (out0, out1, out2, out3))


def first_kernel(
    place_ref, shift_ref, in0, in1, in2, in3, pair_ref, upper_ref, lower_ref, passed_ref, lr, tl, tr, diag
):
    w = tl.shape[0]
    rows, cols = grid_of(w)
    take_in(place_ref, (in0, in1, in2, in3), (tl, tr, diag))
    square = tl[...]
    turned = jnp.transpose(square)
    lr[...] = jnp.where(rows == cols, diag[:1, :], jnp.where(rows > cols, square, turned))
    tl[...] = jnp.where(rows <= cols, square, turned)
    upper_ref[...] = pair_ref[:, :w]
    lower_ref[...] = pair_ref[:, w:]
    inner_rounds(shift_ref, tl, tr, lr, upper_ref, lower_ref, passed_ref.at[w:, :])
    passed_ref[:w, :] = tl[...]


def second_kernel(
    place_ref,
    shifts_ref,
    in0,
    in1,
    in2,
    in3,
    there_ref,
    here_ref,
    lr_ref,
    upper_in,
    lower_in,
    upper_ref,
    lower_ref,
    left,
    right,
    left_turned,
    right_turned,
    tl,
    tr,
    lr,
):
    w = tl.shape[0]
    take_in(place_ref, [piece.at[:, :w] for piece in (in0, in1, in2, in3)], (left,))
    take_in(place_ref, [piece.at[:, w:] for piece in (in0, in1, in2, in3)], (right,))
    replayed_rounds(shifts_ref.at[0], here_ref.at[w:, :], left, right)
    turned = jnp.transpose(right[...])
    left_turned[...] = turned[:, :w]
    right_turned[...] = turned[:, w:]
    replayed_rounds(shifts_ref.at[0], there_ref.at[w:, :], left_turned, right_turned)
    tr[...] = jnp.transpose(left_turned[...])
    tl[...] = there_ref[:w, :]
    lr[...] = lr_ref[...]
    upper_ref[...] = upper_in[...]
    lower_ref[...] = lower_in[...]
    inner_rounds(shifts_ref.at[1], tl, tr, lr, upper_ref, lower_ref)


def passed_along(block, axis, distance):
    devices = range(lax.axis_size(axis))
    route = [((i - distance) % len(devices), i) for i in devices]
    return lax.ppermute(block, axis, route)


def swapped(block, axis, bits):
    return lax.ppermute(block, axis, [(i, i ^ bits) for i in range(lax.axis_size(axis))])


def within_four(outs, axis):
    sent = [swapped(outs[k], axis, k) for k in (3, 1, 2)]
    return (outs[0] + sent[1]) + (sent[2] + sent[0])


def across_fours(mine, axis):
    met = [swapped(mine, axis, k) for k in (8, 4, 12)]
    return (mine + met[1]) + (met[0] + met[2])


def shared_in_four(mine, axis):
    shared = [swapped(mine, axis, k) for k in (3, 1, 2)]
    return (mine, shared[1], shared[2], shared[0])


def per_device(matrix, shifts):
    rows, width = matrix.shape
    w = width // 2
    block = (rows, w)
    square = (w, w)
    diag = (32, w)
    tall = (2 * w, w)
    passed = (w + 2 * shifts.shape[1], w)
    place = (lax.axis_index("row") % 4).astype(jnp.int32).reshape(1)

    other = passed_along(matrix, "col", 2)
    gram = kernel_call(
        gram_kernel, [(2 * w // 4 + 8, w)] * 4, [SMEM, VMEM], [square, square, diag]
    )(place, matrix)
    gram = within_four(gram, "row")
    cross = kernel_call(
        cross_kernel, [(width // 4, width)] * 4, [SMEM, VMEM, VMEM], [(width, width)]
    )(place, other, matrix)
    gram = across_fours(gram, "row")
    cross = within_four(cross, "row")
    gram = shared_in_four(gram, "row")
    cross = across_fours(cross, "row")
    upper, lower, here, lr = kernel_call(
        first_kernel,
        [block, block, passed, square],
        [SMEM, SMEM] + [VMEM] * 5,
        [square, square, diag],
    )(place, shifts[0], *gram, matrix)
    there = passed_along(here, "col", 2)
    upper = passed_along(upper, "col", 2)
    cross = shared_in_four(cross, "row")
    upper, lower = kernel_call(
        second_kernel,
        [block, block],
        [SMEM, SMEM] + [VMEM] * 9,
        [tall, tall] + [square] * 5,
    )(place, shifts, *cross, there, here, lr, upper, lower)
    lower = passed_along(lower, "col", -2)
    return jnp.concatenate([upper, lower], axis=1)


def solution(mesh):
    in_specs = (P("row", "col"), P())
    out_specs = P("row", "col")
    return jax.shard_map(
        per_device, mesh=mesh, in_specs=in_specs, out_specs=out_specs, check_vma=False
    )
```

```python
import jax
import jax.numpy as jnp
from jax import lax
from jax.experimental import pallas as pl
from jax.experimental.pallas import tpu as pltpu
from jax.sharding import PartitionSpec as P

LANES = 128
BLK = 256
VMEM = pl.BlockSpec(memory_space=pltpu.VMEM)
SMEM = pl.BlockSpec(memory_space=pltpu.SMEM)


def kernel_call(kernel, outs, ins, scratch=()):
    return pl.pallas_call(
        kernel,
        out_shape=[jax.ShapeDtypeStruct(shape, jnp.float32) for shape in outs],
        in_specs=ins,
        out_specs=[VMEM] * len(outs),
        scratch_shapes=[pltpu.VMEM(shape, jnp.float32) for shape in scratch],
        compiler_params=pltpu.CompilerParams(vmem_limit_bytes=32 * 1024 * 1024),
    )


def half_angle(x, y):
    scale = jnp.maximum(jnp.abs(x), jnp.abs(y))
    flat = scale == 0.0
    inverse = 1.0 / jnp.where(flat, 1.0, scale)
    xs = x * inverse
    ys = y * inverse
    norm = lax.rsqrt(jnp.where(flat, 1.0, xs * xs + ys * ys))
    major = jnp.sqrt(0.5 + 0.5 * jnp.abs(xs * norm))
    minor = 0.5 * jnp.abs(ys * norm) / major
    negative = (y < 0.0) | ((y == 0.0) & (1.0 / y < 0.0))
    ahead = x >= 0.0
    cosine = jnp.where(flat, 1.0, jnp.where(ahead, major, minor))
    sine = jnp.where(ahead, minor, major)
    sine = jnp.where(negative, -sine, sine)
    return cosine, jnp.where(flat, 0.0, sine)


def grid_of(w):
    rows = lax.broadcasted_iota(jnp.int32, (w, w), 0)
    cols = lax.broadcasted_iota(jnp.int32, (w, w), 1)
    return rows, cols


def diagonal(block):
    rows, cols = grid_of(LANES)
    parts = [
        jnp.sum(jnp.where(rows == cols, block[t : t + LANES, t : t + LANES], 0.0), 0, keepdims=True)
        for t in range(0, block.shape[0], LANES)
    ]
    return jnp.concatenate(parts, axis=1)


def turned_along(vector, back):
    return pltpu.roll(jnp.broadcast_to(vector, (8, vector.shape[1])), back, 1)[:1]


def turns(shift_ref):
    offset = jnp.int32(0)
    for r in range(shift_ref.shape[0]):
        target = shift_ref[r]
        yield r, lax.rem(offset - target + 2 * BLK, BLK)
        offset = target


def inner_rounds(shift_ref, tl, tr, lr, angles_ref):
    w = tl.shape[0]

    def as_rows(vector):
        half = jnp.transpose(jnp.broadcast_to(vector, (LANES, w)))
        return jnp.concatenate([half] * (w // LANES), axis=1)

    a = diagonal(tl[...])
    b = diagonal(lr[...])
    for r, back in turns(shift_ref):
        top_left = tl[...]
        top_right = pltpu.roll(tr[...], back, 1)
        low_right = pltpu.roll(pltpu.roll(lr[...], back, 1), back, 0)
        g = diagonal(top_right)
        b = turned_along(b, back)
        c, s = half_angle(a - b, 2.0 * g)
        angles_ref[2 * r : 2 * r + 1, :] = c
        angles_ref[2 * r + 1 : 2 * r + 2, :] = s
        a, b = (
            (c * a + s * g) * c + (c * g + s * b) * s,
            (c * b - s * g) * c - (c * g - s * a) * s,
        )
        c_rows = as_rows(c)
        s_rows = as_rows(s)
        low_left = jnp.transpose(top_right)
        half_tl = c_rows * top_left + s_rows * low_left
        half_tr = c_rows * top_right + s_rows * low_right
        half_ll = c_rows * low_left - s_rows * top_left
        half_lr = c_rows * low_right - s_rows * top_right
        tl[...] = half_tl * c + half_tr * s
        tr[...] = half_tr * c - half_tl * s
        lr[...] = half_lr * c - half_ll * s
    offset = shift_ref[shift_ref.shape[0] - 1]
    lr[...] = pltpu.roll(pltpu.roll(lr[...], offset, 1), offset, 0)


def rotated(shift_ref, angles_ref, upper_ref, lower_ref):
    for r, back in turns(shift_ref):
        c = angles_ref[2 * r : 2 * r + 1, :]
        s = angles_ref[2 * r + 1 : 2 * r + 2, :]
        upper = upper_ref[...]
        lower = pltpu.roll(lower_ref[...], back, 1)
        upper_ref[...] = upper * c + lower * s
        lower_ref[...] = lower * c - upper * s
    offset = shift_ref[shift_ref.shape[0] - 1]
    lower_ref[...] = pltpu.roll(lower_ref[...], offset, 1)


def full_dot(left, right):
    return lax.dot_general(
        left,
        right,
        (((0,), (0,)), ((), ())),
        precision=lax.Precision.HIGHEST,
        preferred_element_type=jnp.float32,
    )


def hand_out(place_ref, blocks, outs):
    for k, out in enumerate(outs):
        start = 0
        for block in blocks:
            share = block.shape[0] // len(outs)
            quarter = (place_ref[0] ^ k) * share
            out[start : start + share, :] = block[pl.ds(pl.multiple_of(quarter, 8), share), :]
            start += share


def take_in(place_ref, ins, blocks):
    for k, piece in enumerate(ins):
        start = 0
        for block in blocks:
            share = block.shape[0] // len(ins)
            quarter = (place_ref[0] ^ k) * share
            block[pl.ds(pl.multiple_of(quarter, 8), share), :] = piece[start : start + share, :]
            start += share


def gram_kernel(place_ref, pair_ref, out0, out1, out2, out3, square, cross, diag):
    outs = (out0, out1, out2, out3)
    w = pair_ref.shape[1] // 2
    rows, cols = grid_of(w)
    upper = pair_ref[:, :w]
    lower = pair_ref[:, w:]
    low_right = full_dot(lower, lower)
    square[...] = jnp.where(rows <= cols, full_dot(upper, upper), low_right)
    cross[...] = full_dot(upper, lower)
    diag[...] = jnp.broadcast_to(diagonal(low_right), diag.shape)
    hand_out(place_ref, (square, cross, diag), outs)


def first_kernel(
    place_ref, shift_ref, in0, in1, in2, in3, angles_ref, tl, lr, tr, diag
):
    w = tl.shape[0]
    rows, cols = grid_of(w)
    take_in(place_ref, (in0, in1, in2, in3), (tl, tr, diag))
    square = tl[...]
    turned = jnp.transpose(square)
    lr[...] = jnp.where(rows == cols, diag[:1, :], jnp.where(rows > cols, square, turned))
    tl[...] = jnp.where(rows <= cols, square, turned)
    inner_rounds(shift_ref, tl, tr, lr, angles_ref)


def own_kernel(shift_ref, angles_ref, pair_ref, upper_ref, lower_ref):
    w = upper_ref.shape[1]
    upper_ref[...] = pair_ref[:, :w]
    lower_ref[...] = pair_ref[:, w:]
    rotated(shift_ref, angles_ref, upper_ref, lower_ref)


def cross_kernel(
    place_ref, shift_ref, angles_ref, other_ref, lower_ref, upper_ref, out0, out1, out2, out3, rest, cross
):
    w = upper_ref.shape[1]
    upper_ref[...] = other_ref[:, :w]
    rest[...] = other_ref[:, w:]
    rotated(shift_ref, angles_ref, upper_ref, rest)
    cross[...] = full_dot(upper_ref[...], lower_ref[...])
    hand_out(place_ref, (cross,), (out0, out1, out2, out3))


def second_kernel(place_ref, shift_ref, in0, in1, in2, in3, tl_ref, lr_ref, angles_ref, tl, tr, lr):
    tl[...] = tl_ref[...]
    lr[...] = lr_ref[...]
    take_in(place_ref, (in0, in1, in2, in3), (tr,))
    inner_rounds(shift_ref, tl, tr, lr, angles_ref)


def upper_kernel(shift_ref, angles_ref, upper_in, lower_in, upper_ref, rest):
    upper_ref[...] = upper_in[...]
    rest[...] = lower_in[...]
    rotated(shift_ref, angles_ref, upper_ref, rest)


def lower_kernel(shift_ref, angles_ref, upper_in, lower_in, done_ref, pair_ref, upper, lower):
    w = done_ref.shape[1]
    upper[...] = upper_in[...]
    lower[...] = lower_in[...]
    pair_ref[:, :w] = done_ref[...]
    rotated(shift_ref, angles_ref, upper, lower)
    pair_ref[:, w:] = lower[...]


def passed_along(block, axis, distance):
    devices = range(lax.axis_size(axis))
    route = [((i - distance) % len(devices), i) for i in devices]
    return lax.ppermute(block, axis, route)


def swapped(block, axis, bits):
    return lax.ppermute(block, axis, [(i, i ^ bits) for i in range(lax.axis_size(axis))])


def within_four(outs, axis):
    sent = [swapped(outs[k], axis, k) for k in (3, 1, 2)]
    return (outs[0] + sent[1]) + (sent[2] + sent[0])


def across_fours(mine, axis):
    met = [swapped(mine, axis, k) for k in (8, 4, 12)]
    return (mine + met[1]) + (met[0] + met[2])


def shared_in_four(mine, axis):
    shared = [swapped(mine, axis, k) for k in (3, 1, 2)]
    return (mine, shared[1], shared[2], shared[0])


def per_device(matrix, shifts):
    rows, width = matrix.shape
    w = width // 2
    block = (rows, w)
    square = (w, w)
    diag = (32, w)
    angles = (2 * shifts.shape[1], w)
    place = (lax.axis_index("row") % 4).astype(jnp.int32).reshape(1)

    gram = kernel_call(
        gram_kernel, [(2 * w // 4 + 8, w)] * 4, [SMEM, VMEM], [square, square, diag]
    )(place, matrix)
    gram = within_four(gram, "row")
    gram, sent = lax.optimization_barrier((gram, matrix))
    other = passed_along(sent, "col", 2)
    gram = shared_in_four(across_fours(gram, "row"), "row")
    here, tl, lr = kernel_call(
        first_kernel, [angles, square, square], [SMEM, SMEM] + [VMEM] * 4, [square, diag]
    )(place, shifts[0], *gram)
    there = passed_along(here, "col", 2)
    own_upper, lower = kernel_call(own_kernel, [block, block], [SMEM, VMEM, VMEM])(
        shifts[0], here, matrix
    )
    upper, *cross = kernel_call(
        cross_kernel,
        [block] + [(w // 4, w)] * 4,
        [SMEM, SMEM] + [VMEM] * 3,
        [block, square],
    )(place, shifts[0], there, other, lower)
    cross = within_four(cross, "row")
    tl = passed_along(tl, "col", 2)
    far_lower = passed_along(lower, "col", -2)
    cross = shared_in_four(across_fours(cross, "row"), "row")
    (here,) = kernel_call(
        second_kernel, [angles], [SMEM, SMEM] + [VMEM] * 6, [square] * 3
    )(place, shifts[1], *cross, tl, lr)
    there = passed_along(here, "col", -2)
    (upper,) = kernel_call(upper_kernel, [block], [SMEM] + [VMEM] * 3, [block])(
        shifts[1], here, upper, lower
    )
    (pair,) = kernel_call(
        lower_kernel, [(rows, width)], [SMEM] + [VMEM] * 4, [block, block]
    )(shifts[1], there, own_upper, far_lower, upper)
    return pair


def solution(mesh):
    in_specs = (P("row", "col"), P())
    out_specs = P("row", "col")
    return jax.shard_map(
        per_device, mesh=mesh, in_specs=in_specs, out_specs=out_specs, check_vma=False
    )
```

```python
import jax
import jax.numpy as jnp
from jax import lax
from jax.experimental import pallas as pl
from jax.experimental.pallas import tpu as pltpu
from jax.sharding import PartitionSpec as P

LANES = 128
BLK = 256
VMEM = pl.BlockSpec(memory_space=pltpu.VMEM)
SMEM = pl.BlockSpec(memory_space=pltpu.SMEM)


def kernel_call(kernel, outs, ins, scratch=()):
    return pl.pallas_call(
        kernel,
        out_shape=[jax.ShapeDtypeStruct(shape, jnp.float32) for shape in outs],
        in_specs=ins,
        out_specs=[VMEM] * len(outs),
        scratch_shapes=[pltpu.VMEM(shape, jnp.float32) for shape in scratch],
        compiler_params=pltpu.CompilerParams(vmem_limit_bytes=32 * 1024 * 1024),
    )


def half_angle(x, y):
    scale = jnp.maximum(jnp.abs(x), jnp.abs(y))
    flat = scale == 0.0
    inverse = 1.0 / jnp.where(flat, 1.0, scale)
    xs = x * inverse
    ys = y * inverse
    norm = lax.rsqrt(jnp.where(flat, 1.0, xs * xs + ys * ys))
    major = jnp.sqrt(0.5 + 0.5 * jnp.abs(xs * norm))
    minor = 0.5 * jnp.abs(ys * norm) / major
    negative = (y < 0.0) | ((y == 0.0) & (1.0 / y < 0.0))
    ahead = x >= 0.0
    cosine = jnp.where(flat, 1.0, jnp.where(ahead, major, minor))
    sine = jnp.where(ahead, minor, major)
    sine = jnp.where(negative, -sine, sine)
    return cosine, jnp.where(flat, 0.0, sine)


def grid_of(w):
    rows = lax.broadcasted_iota(jnp.int32, (w, w), 0)
    cols = lax.broadcasted_iota(jnp.int32, (w, w), 1)
    return rows, cols


def diagonal(block):
    rows, cols = grid_of(LANES)
    parts = [
        jnp.sum(jnp.where(rows == cols, block[t : t + LANES, t : t + LANES], 0.0), 0, keepdims=True)
        for t in range(0, block.shape[0], LANES)
    ]
    return jnp.concatenate(parts, axis=1)


def turned_along(vector, back):
    return pltpu.roll(jnp.broadcast_to(vector, (8, vector.shape[1])), back, 1)[:1]


def turns(shift_ref):
    offset = jnp.int32(0)
    for r in range(shift_ref.shape[0]):
        target = shift_ref[r]
        yield r, lax.rem(offset - target + 2 * BLK, BLK)
        offset = target


def inner_rounds(shift_ref, tl, tr, lr, angles_ref, keep=False):
    w = tl.shape[0]

    def as_rows(vector):
        half = jnp.transpose(jnp.broadcast_to(vector, (LANES, w)))
        return jnp.concatenate([half] * (w // LANES), axis=1)

    a = diagonal(tl[...])
    b = diagonal(lr[...])
    for r, back in turns(shift_ref):
        top_left = tl[...]
        top_right = pltpu.roll(tr[...], back, 1)
        low_right = pltpu.roll(pltpu.roll(lr[...], back, 1), back, 0)
        g = diagonal(top_right)
        b = turned_along(b, back)
        c, s = half_angle(a - b, 2.0 * g)
        angles_ref[2 * r : 2 * r + 1, :] = c
        angles_ref[2 * r + 1 : 2 * r + 2, :] = s
        a, b = (
            (c * a + s * g) * c + (c * g + s * b) * s,
            (c * b - s * g) * c - (c * g - s * a) * s,
        )
        left = shift_ref.shape[0] - 1 - r
        if left == 0 and not keep:
            break
        c_rows = as_rows(c)
        s_rows = as_rows(s)
        low_left = jnp.transpose(top_right)
        half_tl = c_rows * top_left + s_rows * low_left
        half_tr = c_rows * top_right + s_rows * low_right
        half_ll = c_rows * low_left - s_rows * top_left
        half_lr = c_rows * low_right - s_rows * top_right
        if left > 0:
            tr[...] = half_tr * c - half_tl * s
        if left > 1 or keep:
            tl[...] = half_tl * c + half_tr * s
            lr[...] = half_lr * c - half_ll * s
    if keep:
        offset = shift_ref[shift_ref.shape[0] - 1]
        lr[...] = pltpu.roll(pltpu.roll(lr[...], offset, 1), offset, 0)


def rotated(shift_ref, angles_ref, upper_ref, lower_ref):
    for r, back in turns(shift_ref):
        c = angles_ref[2 * r : 2 * r + 1, :]
        s = angles_ref[2 * r + 1 : 2 * r + 2, :]
        upper = upper_ref[...]
        lower = pltpu.roll(lower_ref[...], back, 1)
        upper_ref[...] = upper * c + lower * s
        lower_ref[...] = lower * c - upper * s
    offset = shift_ref[shift_ref.shape[0] - 1]
    lower_ref[...] = pltpu.roll(lower_ref[...], offset, 1)


def full_dot(left, right):
    return lax.dot_general(
        left,
        right,
        (((0,), (0,)), ((), ())),
        precision=lax.Precision.HIGHEST,
        preferred_element_type=jnp.float32,
    )


def hand_out(place_ref, blocks, outs):
    for k, out in enumerate(outs):
        start = 0
        for block in blocks:
            share = block.shape[0] // len(outs)
            quarter = (place_ref[0] ^ k) * share
            out[start : start + share, :] = block[pl.ds(pl.multiple_of(quarter, 8), share), :]
            start += share


def take_in(place_ref, ins, blocks):
    for k, piece in enumerate(ins):
        start = 0
        for block in blocks:
            share = block.shape[0] // len(ins)
            quarter = (place_ref[0] ^ k) * share
            block[pl.ds(pl.multiple_of(quarter, 8), share), :] = piece[start : start + share, :]
            start += share


def gram_kernel(place_ref, pair_ref, out0, out1, out2, out3, square, cross, diag):
    outs = (out0, out1, out2, out3)
    w = pair_ref.shape[1] // 2
    rows, cols = grid_of(w)
    upper = pair_ref[:, :w]
    lower = pair_ref[:, w:]
    low_right = full_dot(lower, lower)
    square[...] = jnp.where(rows <= cols, full_dot(upper, upper), low_right)
    cross[...] = full_dot(upper, lower)
    diag[...] = jnp.broadcast_to(diagonal(low_right), diag.shape)
    hand_out(place_ref, (square, cross, diag), outs)


def first_kernel(
    place_ref, shift_ref, in0, in1, in2, in3, angles_ref, tl, lr, tr, diag
):
    w = tl.shape[0]
    rows, cols = grid_of(w)
    take_in(place_ref, (in0, in1, in2, in3), (tl, tr, diag))
    square = tl[...]
    turned = jnp.transpose(square)
    lr[...] = jnp.where(rows == cols, diag[:1, :], jnp.where(rows > cols, square, turned))
    tl[...] = jnp.where(rows <= cols, square, turned)
    inner_rounds(shift_ref, tl, tr, lr, angles_ref, keep=True)


def own_kernel(shift_ref, angles_ref, pair_ref, upper_ref, lower_ref):
    w = upper_ref.shape[1]
    upper_ref[...] = pair_ref[:, :w]
    lower_ref[...] = pair_ref[:, w:]
    rotated(shift_ref, angles_ref, upper_ref, lower_ref)


def cross_kernel(
    place_ref, shift_ref, angles_ref, other_ref, lower_ref, upper_ref, out0, out1, out2, out3, rest, cross
):
    w = upper_ref.shape[1]
    upper_ref[...] = other_ref[:, :w]
    rest[...] = other_ref[:, w:]
    rotated(shift_ref, angles_ref, upper_ref, rest)
    cross[...] = full_dot(upper_ref[...], lower_ref[...])
    hand_out(place_ref, (cross,), (out0, out1, out2, out3))


def second_kernel(place_ref, shift_ref, in0, in1, in2, in3, tl_ref, lr_ref, angles_ref, tl, tr, lr):
    tl[...] = tl_ref[...]
    lr[...] = lr_ref[...]
    take_in(place_ref, (in0, in1, in2, in3), (tr,))
    inner_rounds(shift_ref, tl, tr, lr, angles_ref)


def upper_kernel(shift_ref, angles_ref, upper_in, lower_in, upper_ref, rest):
    upper_ref[...] = upper_in[...]
    rest[...] = lower_in[...]
    rotated(shift_ref, angles_ref, upper_ref, rest)


def lower_kernel(shift_ref, angles_ref, upper_in, lower_in, done_ref, pair_ref, upper, lower):
    w = done_ref.shape[1]
    upper[...] = upper_in[...]
    lower[...] = lower_in[...]
    pair_ref[:, :w] = done_ref[...]
    rotated(shift_ref, angles_ref, upper, lower)
    pair_ref[:, w:] = lower[...]


def passed_along(block, axis, distance):
    devices = range(lax.axis_size(axis))
    route = [((i - distance) % len(devices), i) for i in devices]
    return lax.ppermute(block, axis, route)


def swapped(block, axis, bits):
    return lax.ppermute(block, axis, [(i, i ^ bits) for i in range(lax.axis_size(axis))])


def within_four(outs, axis):
    sent = [swapped(outs[k], axis, k) for k in (3, 1, 2)]
    return (outs[0] + sent[1]) + (sent[2] + sent[0])


def across_fours(mine, axis):
    met = [swapped(mine, axis, k) for k in (8, 4, 12)]
    return (mine + met[1]) + (met[0] + met[2])


def met_across(mine, axis):
    h = mine.shape[0] // 2 // 8 * 8
    a, b = mine[:h], mine[h:]
    a1, b1 = swapped(a, axis, 4), swapped(b, axis, 12)
    a, b = a + a1, b + b1
    a1, b1 = swapped(a, axis, 12), swapped(b, axis, 4)
    return jnp.concatenate([a + a1, b + b1], axis=0)


def shared_in_four(mine, axis):
    shared = [swapped(mine, axis, k) for k in (3, 1, 2)]
    return (mine, shared[1], shared[2], shared[0])


def per_device(matrix, shifts):
    rows, width = matrix.shape
    w = width // 2
    block = (rows, w)
    square = (w, w)
    diag = (32, w)
    angles = (2 * shifts.shape[1], w)
    place = (lax.axis_index("row") % 4).astype(jnp.int32).reshape(1)

    gram = kernel_call(
        gram_kernel, [(2 * w // 4 + 8, w)] * 4, [SMEM, VMEM], [square, square, diag]
    )(place, matrix)
    gram = within_four(gram, "row")
    gram, sent = lax.optimization_barrier((gram, matrix))
    other = passed_along(sent, "col", 2)
    gram = shared_in_four(met_across(gram, "row"), "row")
    here, tl, lr = kernel_call(
        first_kernel, [angles, square, square], [SMEM, SMEM] + [VMEM] * 4, [square, diag]
    )(place, shifts[0], *gram)
    there = passed_along(here, "col", 2)
    own_upper, lower = kernel_call(own_kernel, [block, block], [SMEM, VMEM, VMEM])(
        shifts[0], here, matrix
    )
    upper, *cross = kernel_call(
        cross_kernel,
        [block] + [(w // 4, w)] * 4,
        [SMEM, SMEM] + [VMEM] * 3,
        [block, square],
    )(place, shifts[0], there, other, lower)
    cross = within_four(cross, "row")
    tl = passed_along(tl, "col", 2)
    far_lower = passed_along(lower, "col", -2)
    cross = shared_in_four(across_fours(cross, "row"), "row")
    (here,) = kernel_call(
        second_kernel, [angles], [SMEM, SMEM] + [VMEM] * 6, [square] * 3
    )(place, shifts[1], *cross, tl, lr)
    there = passed_along(here, "col", -2)
    (upper,) = kernel_call(upper_kernel, [block], [SMEM] + [VMEM] * 3, [block])(
        shifts[1], here, upper, lower
    )
    (pair,) = kernel_call(
        lower_kernel, [(rows, width)], [SMEM] + [VMEM] * 4, [block, block]
    )(shifts[1], there, own_upper, far_lower, upper)
    return pair


def solution(mesh):
    in_specs = (P("row", "col"), P())
    out_specs = P("row", "col")
    return jax.shard_map(
        per_device, mesh=mesh, in_specs=in_specs, out_specs=out_specs, check_vma=False
    )
```

```python
import jax
import jax.numpy as jnp
from jax import lax
from jax.experimental import pallas as pl
from jax.experimental.pallas import tpu as pltpu
from jax.sharding import PartitionSpec as P

LANES = 128
BLK = 256
VMEM = pl.BlockSpec(memory_space=pltpu.VMEM)
SMEM = pl.BlockSpec(memory_space=pltpu.SMEM)
ANY = pl.BlockSpec(memory_space=pl.ANY)


def kernel_call(kernel, outs, ins, scratch=()):
    return pl.pallas_call(
        kernel,
        out_shape=[jax.ShapeDtypeStruct(shape, jnp.float32) for shape in outs],
        in_specs=ins,
        out_specs=[VMEM] * len(outs),
        scratch_shapes=[pltpu.VMEM(shape, jnp.float32) for shape in scratch],
        compiler_params=pltpu.CompilerParams(vmem_limit_bytes=32 * 1024 * 1024),
    )


def output_call(kernel, like, ins, scratch, aliases={}):
    return pl.pallas_call(
        kernel,
        out_shape=jax.ShapeDtypeStruct(like.shape, jnp.float32),
        in_specs=[SMEM] + ins,
        out_specs=ANY,
        scratch_shapes=[pltpu.VMEM(shape, jnp.float32) for shape in scratch]
        + [pltpu.SemaphoreType.DMA],
        input_output_aliases=aliases,
        compiler_params=pltpu.CompilerParams(vmem_limit_bytes=32 * 1024 * 1024),
    )


def half_angle(x, y):
    scale = jnp.maximum(jnp.abs(x), jnp.abs(y))
    flat = scale == 0.0
    inverse = 1.0 / jnp.where(flat, 1.0, scale)
    xs = x * inverse
    ys = y * inverse
    norm = lax.rsqrt(jnp.where(flat, 1.0, xs * xs + ys * ys))
    major = jnp.sqrt(0.5 + 0.5 * jnp.abs(xs * norm))
    minor = 0.5 * jnp.abs(ys * norm) / major
    negative = (y < 0.0) | ((y == 0.0) & (1.0 / y < 0.0))
    ahead = x >= 0.0
    cosine = jnp.where(flat, 1.0, jnp.where(ahead, major, minor))
    sine = jnp.where(ahead, minor, major)
    sine = jnp.where(negative, -sine, sine)
    return cosine, jnp.where(flat, 0.0, sine)


def grid_of(w):
    rows = lax.broadcasted_iota(jnp.int32, (w, w), 0)
    cols = lax.broadcasted_iota(jnp.int32, (w, w), 1)
    return rows, cols


def diagonal(block):
    rows, cols = grid_of(LANES)
    parts = [
        jnp.sum(jnp.where(rows == cols, block[t : t + LANES, t : t + LANES], 0.0), 0, keepdims=True)
        for t in range(0, block.shape[0], LANES)
    ]
    return jnp.concatenate(parts, axis=1)


def turned_along(vector, back):
    return pltpu.roll(jnp.broadcast_to(vector, (8, vector.shape[1])), back, 1)[:1]


def as_rows(vector):
    w = vector.shape[1]
    half = jnp.transpose(jnp.broadcast_to(vector, (LANES, w)))
    return jnp.concatenate([half] * (w // LANES), axis=1)


def turns(shift_ref):
    offset = jnp.int32(0)
    for r in range(shift_ref.shape[0]):
        target = shift_ref[r]
        yield r, lax.rem(offset - target + 2 * BLK, BLK)
        offset = target


def inner_rounds(shift_ref, tl, tr, lr, angles_ref, finished_later=False):
    w = tl.shape[0]

    a = diagonal(tl[...])
    b = diagonal(lr[...])
    for r, back in turns(shift_ref):
        top_left = tl[...]
        top_right = pltpu.roll(tr[...], back, 1)
        low_right = pltpu.roll(pltpu.roll(lr[...], back, 1), back, 0)
        g = diagonal(top_right)
        b = turned_along(b, back)
        c, s = half_angle(a - b, 2.0 * g)
        angles_ref[2 * r : 2 * r + 1, :] = c
        angles_ref[2 * r + 1 : 2 * r + 2, :] = s
        a, b = (
            (c * a + s * g) * c + (c * g + s * b) * s,
            (c * b - s * g) * c - (c * g - s * a) * s,
        )
        left = shift_ref.shape[0] - 1 - r
        if left == 0:
            break
        c_rows = as_rows(c)
        s_rows = as_rows(s)
        low_left = jnp.transpose(top_right)
        half_tl = c_rows * top_left + s_rows * low_left
        half_tr = c_rows * top_right + s_rows * low_right
        half_ll = c_rows * low_left - s_rows * top_left
        half_lr = c_rows * low_right - s_rows * top_right
        tr[...] = half_tr * c - half_tl * s
        if left > 1 or finished_later:
            tl[...] = half_tl * c + half_tr * s
            lr[...] = half_lr * c - half_ll * s


def last_update(shift_ref, angles_ref, tl, tr, lr):
    w = tl.shape[0]
    last = shift_ref.shape[0] - 1
    back = lax.rem(shift_ref[last - 1] - shift_ref[last] + 2 * BLK, BLK)
    c = angles_ref[2 * last : 2 * last + 1, :]
    s = angles_ref[2 * last + 1 : 2 * last + 2, :]
    c_rows = as_rows(c)
    s_rows = as_rows(s)
    top_left = tl[...]
    top_right = pltpu.roll(tr[...], back, 1)
    low_left = jnp.transpose(top_right)
    low_right = pltpu.roll(pltpu.roll(lr[...], back, 1), back, 0)
    half_tl = c_rows * top_left + s_rows * low_left
    half_tr = c_rows * top_right + s_rows * low_right
    half_ll = c_rows * low_left - s_rows * top_left
    half_lr = c_rows * low_right - s_rows * top_right
    offset = shift_ref[last]
    low_right = half_lr * c - half_ll * s
    return (
        half_tl * c + half_tr * s,
        pltpu.roll(pltpu.roll(low_right, offset, 1), offset, 0),
    )


def rotated(shift_ref, angles_ref, upper_ref, lower_ref):
    for r, back in turns(shift_ref):
        c = angles_ref[2 * r : 2 * r + 1, :]
        s = angles_ref[2 * r + 1 : 2 * r + 2, :]
        upper = upper_ref[...]
        lower = pltpu.roll(lower_ref[...], back, 1)
        upper_ref[...] = upper * c + lower * s
        lower_ref[...] = lower * c - upper * s
    offset = shift_ref[shift_ref.shape[0] - 1]
    lower_ref[...] = pltpu.roll(lower_ref[...], offset, 1)


def full_dot(left, right):
    return lax.dot_general(
        left,
        right,
        (((0,), (0,)), ((), ())),
        precision=lax.Precision.HIGHEST,
        preferred_element_type=jnp.float32,
    )


def hand_out(place_ref, blocks, outs):
    for k, out in enumerate(outs):
        start = 0
        for block in blocks:
            share = block.shape[0] // len(outs)
            quarter = (place_ref[0] ^ k) * share
            out[start : start + share, :] = block[pl.ds(pl.multiple_of(quarter, 8), share), :]
            start += share


def take_in(place_ref, ins, blocks):
    for k, piece in enumerate(ins):
        start = 0
        for block in blocks:
            share = block.shape[0] // len(ins)
            quarter = (place_ref[0] ^ k) * share
            block[pl.ds(pl.multiple_of(quarter, 8), share), :] = piece[start : start + share, :]
            start += share


def gram_kernel(place_ref, pair_ref, out0, out1, out2, out3, square, cross, diag):
    outs = (out0, out1, out2, out3)
    w = pair_ref.shape[1] // 2
    rows, cols = grid_of(w)
    upper = pair_ref[:, :w]
    lower = pair_ref[:, w:]
    low_right = full_dot(lower, lower)
    square[...] = jnp.where(rows <= cols, full_dot(upper, upper), low_right)
    cross[...] = full_dot(upper, lower)
    diag[...] = jnp.broadcast_to(diagonal(low_right), diag.shape)
    hand_out(place_ref, (square, cross, diag), outs)


def first_kernel(
    place_ref, shift_ref, in0, in1, in2, in3, angles_ref, tl, tr, lr, diag
):
    w = tl.shape[0]
    rows, cols = grid_of(w)
    take_in(place_ref, (in0, in1, in2, in3), (tl, tr, diag))
    square = tl[...]
    turned = jnp.transpose(square)
    lr[...] = jnp.where(rows == cols, diag[:1, :], jnp.where(rows > cols, square, turned))
    tl[...] = jnp.where(rows <= cols, square, turned)
    inner_rounds(shift_ref, tl, tr, lr, angles_ref, finished_later=True)


def last_kernel(shift_ref, angles_ref, tl, tr, lr, tl_ref, lr_ref):
    top_left, lr_ref[...] = last_update(shift_ref, angles_ref, tl, tr, lr)
    tl_ref[...] = packed(top_left)


def own_kernel(shift_ref, angles_ref, pair_ref, upper_ref, lower_ref):
    w = upper_ref.shape[1]
    upper_ref[...] = pair_ref[:, :w]
    lower_ref[...] = pair_ref[:, w:]
    rotated(shift_ref, angles_ref, upper_ref, lower_ref)


def cross_kernel(
    place_ref, shift_ref, angles_ref, other_ref, lower_ref, upper_ref, out0, out1, out2, out3, rest, cross
):
    w = upper_ref.shape[1]
    upper_ref[...] = other_ref[:, :w]
    rest[...] = other_ref[:, w:]
    rotated(shift_ref, angles_ref, upper_ref, rest)
    cross[...] = full_dot(upper_ref[...], lower_ref[...])
    hand_out(place_ref, (cross,), (out0, out1, out2, out3))


def packed(block):
    h = block.shape[0] // 2
    q = h // 2
    low = block[h:, h:]
    return jnp.concatenate([block[:h], jnp.concatenate([low[:q], low[q:]], axis=1)], axis=0)


def unpacked(parts):
    h = parts.shape[1] // 2
    q = h // 2
    top = parts[:h]
    low = jnp.concatenate([parts[h:, :h], parts[h:, h:]], axis=0)
    low = jnp.concatenate([jnp.transpose(top[:, h:]), low], axis=1)
    return jnp.concatenate([top, low], axis=0)


def second_kernel(place_ref, shift_ref, in0, in1, in2, in3, tl_ref, lr_ref, angles_ref, tl, tr, lr):
    tl[...] = unpacked(tl_ref[...])
    lr[...] = lr_ref[...]
    take_in(place_ref, (in0, in1, in2, in3), (tr,))
    inner_rounds(shift_ref, tl, tr, lr, angles_ref)


def upper_kernel(shift_ref, angles_ref, upper_in, lower_in, pair_ref, upper, rest, sem):
    upper[...] = upper_in[...]
    rest[...] = lower_in[...]
    rotated(shift_ref, angles_ref, upper, rest)
    copy = pltpu.make_async_copy(upper, pair_ref.at[:, : upper.shape[1]], sem)
    copy.start()
    copy.wait()


def lower_kernel(shift_ref, angles_ref, upper_in, lower_in, half_ref, pair_ref, done, sem):
    w = done.shape[1]
    rounds = list(turns(shift_ref))
    for t in range(0, done.shape[0], 8):
        upper = upper_in[t : t + 8, :]
        lower = lower_in[t : t + 8, :]
        for r, back in rounds:
            c = angles_ref[2 * r : 2 * r + 1, :]
            s = angles_ref[2 * r + 1 : 2 * r + 2, :]
            lower = pltpu.roll(lower, back, 1)
            upper, lower = upper * c + lower * s, lower * c - upper * s
        done[t : t + 8, :] = pltpu.roll(lower, shift_ref[shift_ref.shape[0] - 1], 1)
    copy = pltpu.make_async_copy(done, pair_ref.at[:, w:], sem)
    copy.start()
    copy.wait()


def passed_along(block, axis, distance):
    devices = range(lax.axis_size(axis))
    route = [((i - distance) % len(devices), i) for i in devices]
    return lax.ppermute(block, axis, route)


def swapped(block, axis, bits):
    return lax.ppermute(block, axis, [(i, i ^ bits) for i in range(lax.axis_size(axis))])


def within_four(outs, axis):
    sent = [swapped(outs[k], axis, k) for k in (3, 1, 2)]
    return (outs[0] + sent[1]) + (sent[2] + sent[0])


def across_fours(mine, axis):
    met = [swapped(mine, axis, k) for k in (8, 4, 12)]
    return (mine + met[1]) + (met[0] + met[2])


def met_across(mine, axis):
    h = mine.shape[0] // 2 // 8 * 8
    a, b = mine[:h], mine[h:]
    a1, b1 = swapped(a, axis, 4), swapped(b, axis, 12)
    a, b = a + a1, b + b1
    a1, b1 = swapped(a, axis, 12), swapped(b, axis, 4)
    return jnp.concatenate([a + a1, b + b1], axis=0)


def shared_in_four(mine, axis):
    shared = [swapped(mine, axis, k) for k in (3, 1, 2)]
    return (mine, shared[1], shared[2], shared[0])


def per_device(matrix, shifts):
    rows, width = matrix.shape
    w = width // 2
    block = (rows, w)
    square = (w, w)
    diag = (32, w)
    angles = (2 * shifts.shape[1], w)
    place = (lax.axis_index("row") % 4).astype(jnp.int32).reshape(1)

    gram = kernel_call(
        gram_kernel, [(2 * w // 4 + 8, w)] * 4, [SMEM, VMEM], [square, square, diag]
    )(place, matrix)
    gram = within_four(gram, "row")
    gram, sent = lax.optimization_barrier((gram, matrix))
    other = passed_along(sent, "col", 2)
    gram = shared_in_four(met_across(gram, "row"), "row")
    here, *state = kernel_call(
        first_kernel, [angles] + [square] * 3, [SMEM, SMEM] + [VMEM] * 4, [diag]
    )(place, shifts[0], *gram)
    there = passed_along(here, "col", 2)
    own_upper, lower = kernel_call(own_kernel, [block, block], [SMEM, VMEM, VMEM])(
        shifts[0], here, matrix
    )
    tl, lr = kernel_call(last_kernel, [(3 * w // 4, w), square], [SMEM] + [VMEM] * 4)(
        shifts[0], here, *state
    )
    upper, *cross = kernel_call(
        cross_kernel,
        [block] + [(w // 4, w)] * 4,
        [SMEM, SMEM] + [VMEM] * 3,
        [block, square],
    )(place, shifts[0], there, other, lower)
    cross = within_four(cross, "row")
    tl = passed_along(tl, "col", 2)
    tl, sent = lax.optimization_barrier((tl, lower))
    far_lower = passed_along(sent, "col", -2)
    cross = shared_in_four(across_fours(cross, "row"), "row")
    (here,) = kernel_call(
        second_kernel, [angles], [SMEM, SMEM] + [VMEM] * 6, [square] * 3
    )(place, shifts[1], *cross, tl, lr)
    there = passed_along(here, "col", -2)
    half = output_call(upper_kernel, matrix, [VMEM] * 3, [block, block])(
        shifts[1], here, upper, lower
    )
    return output_call(lower_kernel, matrix, [VMEM] * 3 + [ANY], [block], {4: 0})(
        shifts[1], there, own_upper, far_lower, half
    )


def solution(mesh):
    in_specs = (P("row", "col"), P())
    out_specs = P("row", "col")
    return jax.shard_map(
        per_device, mesh=mesh, in_specs=in_specs, out_specs=out_specs, check_vma=False
    )
```

```python
import jax
import jax.numpy as jnp
from jax import lax
from jax.experimental import pallas as pl
from jax.experimental.pallas import tpu as pltpu
from jax.sharding import PartitionSpec as P

LANES = 128
BLK = 256
VMEM = pl.BlockSpec(memory_space=pltpu.VMEM)
SMEM = pl.BlockSpec(memory_space=pltpu.SMEM)
ANY = pl.BlockSpec(memory_space=pl.ANY)


def kernel_call(kernel, outs, ins, scratch=()):
    return pl.pallas_call(
        kernel,
        out_shape=[jax.ShapeDtypeStruct(shape, jnp.float32) for shape in outs],
        in_specs=ins,
        out_specs=[VMEM] * len(outs),
        scratch_shapes=[pltpu.VMEM(shape, jnp.float32) for shape in scratch],
        compiler_params=pltpu.CompilerParams(vmem_limit_bytes=32 * 1024 * 1024),
    )


def output_call(kernel, like, ins, scratch, aliases={}):
    return pl.pallas_call(
        kernel,
        out_shape=jax.ShapeDtypeStruct(like.shape, jnp.float32),
        in_specs=[SMEM] + ins,
        out_specs=ANY,
        scratch_shapes=[pltpu.VMEM(shape, jnp.float32) for shape in scratch]
        + [pltpu.SemaphoreType.DMA],
        input_output_aliases=aliases,
        compiler_params=pltpu.CompilerParams(vmem_limit_bytes=32 * 1024 * 1024),
    )


def half_angle(x, y):
    scale = jnp.maximum(jnp.abs(x), jnp.abs(y))
    flat = scale == 0.0
    inverse = 1.0 / jnp.where(flat, 1.0, scale)
    xs = x * inverse
    ys = y * inverse
    norm = lax.rsqrt(jnp.where(flat, 1.0, xs * xs + ys * ys))
    major = jnp.sqrt(0.5 + 0.5 * jnp.abs(xs * norm))
    minor = 0.5 * jnp.abs(ys * norm) / major
    negative = (y < 0.0) | ((y == 0.0) & (1.0 / y < 0.0))
    ahead = x >= 0.0
    cosine = jnp.where(flat, 1.0, jnp.where(ahead, major, minor))
    sine = jnp.where(ahead, minor, major)
    sine = jnp.where(negative, -sine, sine)
    return cosine, jnp.where(flat, 0.0, sine)


def grid_of(w):
    rows = lax.broadcasted_iota(jnp.int32, (w, w), 0)
    cols = lax.broadcasted_iota(jnp.int32, (w, w), 1)
    return rows, cols


def diagonal(block):
    rows, cols = grid_of(LANES)
    parts = [
        jnp.sum(jnp.where(rows == cols, block[t : t + LANES, t : t + LANES], 0.0), 0, keepdims=True)
        for t in range(0, block.shape[0], LANES)
    ]
    return jnp.concatenate(parts, axis=1)


def turned_along(vector, back):
    return pltpu.roll(jnp.broadcast_to(vector, (8, vector.shape[1])), back, 1)[:1]


def as_rows(vector):
    w = vector.shape[1]
    half = jnp.transpose(jnp.broadcast_to(vector, (LANES, w)))
    return jnp.concatenate([half] * (w // LANES), axis=1)


def turns(shift_ref):
    offset = jnp.int32(0)
    for r in range(shift_ref.shape[0]):
        target = shift_ref[r]
        yield r, lax.rem(offset - target + 2 * BLK, BLK)
        offset = target


def inner_rounds(shift_ref, tl, tr, lr, angles_ref, finished_later=False):
    w = tl.shape[0]

    a = diagonal(tl[...])
    b = diagonal(lr[...])
    for r, back in turns(shift_ref):
        top_left = tl[...]
        top_right = pltpu.roll(tr[...], back, 1)
        low_right = pltpu.roll(pltpu.roll(lr[...], back, 1), back, 0)
        g = diagonal(top_right)
        b = turned_along(b, back)
        c, s = half_angle(a - b, 2.0 * g)
        angles_ref[2 * r : 2 * r + 1, :] = c
        angles_ref[2 * r + 1 : 2 * r + 2, :] = s
        a, b = (
            (c * a + s * g) * c + (c * g + s * b) * s,
            (c * b - s * g) * c - (c * g - s * a) * s,
        )
        left = shift_ref.shape[0] - 1 - r
        if left == 0:
            break
        c_rows = as_rows(c)
        s_rows = as_rows(s)
        low_left = jnp.transpose(top_right)
        half_tl = c_rows * top_left + s_rows * low_left
        half_tr = c_rows * top_right + s_rows * low_right
        half_ll = c_rows * low_left - s_rows * top_left
        half_lr = c_rows * low_right - s_rows * top_right
        tr[...] = half_tr * c - half_tl * s
        if left > 1 or finished_later:
            tl[...] = half_tl * c + half_tr * s
            lr[...] = half_lr * c - half_ll * s


def last_update(shift_ref, angles_ref, tl, tr, lr):
    w = tl.shape[0]
    last = shift_ref.shape[0] - 1
    back = lax.rem(shift_ref[last - 1] - shift_ref[last] + 2 * BLK, BLK)
    c = angles_ref[2 * last : 2 * last + 1, :]
    s = angles_ref[2 * last + 1 : 2 * last + 2, :]
    c_rows = as_rows(c)
    s_rows = as_rows(s)
    top_left = tl[...]
    top_right = pltpu.roll(tr[...], back, 1)
    low_left = jnp.transpose(top_right)
    low_right = pltpu.roll(pltpu.roll(lr[...], back, 1), back, 0)
    half_tl = c_rows * top_left + s_rows * low_left
    half_tr = c_rows * top_right + s_rows * low_right
    half_ll = c_rows * low_left - s_rows * top_left
    half_lr = c_rows * low_right - s_rows * top_right
    offset = shift_ref[last]
    low_right = half_lr * c - half_ll * s
    return (
        half_tl * c + half_tr * s,
        pltpu.roll(pltpu.roll(low_right, offset, 1), offset, 0),
    )


def rotated(shift_ref, angles_ref, upper_ref, lower_ref):
    for r, back in turns(shift_ref):
        c = angles_ref[2 * r : 2 * r + 1, :]
        s = angles_ref[2 * r + 1 : 2 * r + 2, :]
        upper = upper_ref[...]
        lower = pltpu.roll(lower_ref[...], back, 1)
        upper_ref[...] = upper * c + lower * s
        lower_ref[...] = lower * c - upper * s
    offset = shift_ref[shift_ref.shape[0] - 1]
    lower_ref[...] = pltpu.roll(lower_ref[...], offset, 1)


def full_dot(left, right):
    return lax.dot_general(
        left,
        right,
        (((0,), (0,)), ((), ())),
        precision=lax.Precision.HIGHEST,
        preferred_element_type=jnp.float32,
    )


def hand_out(place_ref, blocks, outs):
    for k, out in enumerate(outs):
        start = 0
        for block in blocks:
            share = block.shape[0] // len(outs)
            quarter = (place_ref[0] ^ k) * share
            out[start : start + share, :] = block[pl.ds(pl.multiple_of(quarter, 8), share), :]
            start += share


def take_in(place_ref, ins, blocks):
    for k, piece in enumerate(ins):
        start = 0
        for block in blocks:
            share = block.shape[0] // len(ins)
            quarter = (place_ref[0] ^ k) * share
            block[pl.ds(pl.multiple_of(quarter, 8), share), :] = piece[start : start + share, :]
            start += share


def gram_kernel(place_ref, pair_ref, out0, out1, out2, out3, square, cross, diag):
    outs = (out0, out1, out2, out3)
    w = pair_ref.shape[1] // 2
    rows, cols = grid_of(w)
    upper = pair_ref[:, :w]
    lower = pair_ref[:, w:]
    low_right = full_dot(lower, lower)
    square[...] = jnp.where(rows <= cols, full_dot(upper, upper), low_right)
    cross[...] = full_dot(upper, lower)
    diag[...] = jnp.broadcast_to(diagonal(low_right), diag.shape)
    hand_out(place_ref, (square, cross, diag), outs)


def first_kernel(
    place_ref, shift_ref, in0, in1, in2, in3, angles_ref, tl, tr, lr, diag
):
    w = tl.shape[0]
    rows, cols = grid_of(w)
    take_in(place_ref, (in0, in1, in2, in3), (tl, tr, diag))
    square = tl[...]
    turned = jnp.transpose(square)
    lr[...] = jnp.where(rows == cols, diag[:1, :], jnp.where(rows > cols, square, turned))
    tl[...] = jnp.where(rows <= cols, square, turned)
    inner_rounds(shift_ref, tl, tr, lr, angles_ref, finished_later=True)


def last_kernel(shift_ref, angles_ref, tl, tr, lr, tl_ref, lr_ref):
    top_left, lr_ref[...] = last_update(shift_ref, angles_ref, tl, tr, lr)
    tl_ref[...] = packed(top_left)


def own_kernel(shift_ref, angles_ref, pair_ref, upper_ref, lower_ref):
    w = upper_ref.shape[1]
    upper_ref[...] = pair_ref[:, :w]
    lower_ref[...] = pair_ref[:, w:]
    rotated(shift_ref, angles_ref, upper_ref, lower_ref)


def cross_kernel(
    place_ref, shift_ref, angles_ref, other_ref, lower_ref, upper_ref, out0, out1, out2, out3, rest, cross
):
    w = upper_ref.shape[1]
    upper_ref[...] = other_ref[:, :w]
    rest[...] = other_ref[:, w:]
    rotated(shift_ref, angles_ref, upper_ref, rest)
    cross[...] = full_dot(upper_ref[...], lower_ref[...])
    hand_out(place_ref, (cross,), (out0, out1, out2, out3))


def packed(block):
    h = block.shape[0] // 2
    q = h // 2
    low = block[h:, h:]
    return jnp.concatenate([block[:h], jnp.concatenate([low[:q], low[q:]], axis=1)], axis=0)


def unpacked(parts):
    h = parts.shape[1] // 2
    q = h // 2
    top = parts[:h]
    low = jnp.concatenate([parts[h:, :h], parts[h:, h:]], axis=0)
    low = jnp.concatenate([jnp.transpose(top[:, h:]), low], axis=1)
    return jnp.concatenate([top, low], axis=0)


def second_kernel(place_ref, shift_ref, in0, in1, in2, in3, tl_ref, lr_ref, angles_ref, tl, tr, lr):
    tl[...] = unpacked(tl_ref[...])
    lr[...] = lr_ref[...]
    take_in(place_ref, (in0, in1, in2, in3), (tr,))
    inner_rounds(shift_ref, tl, tr, lr, angles_ref)


def upper_kernel(shift_ref, angles_ref, upper_in, lower_in, pair_ref, upper, rest, sem):
    upper[...] = upper_in[...]
    rest[...] = lower_in[...]
    rotated(shift_ref, angles_ref, upper, rest)
    copy = pltpu.make_async_copy(upper, pair_ref.at[:, : upper.shape[1]], sem)
    copy.start()
    copy.wait()


def lower_kernel(shift_ref, angles_ref, upper_in, lower_in, half_ref, pair_ref, done, sem):
    w = done.shape[1]
    rounds = list(turns(shift_ref))
    for t in range(0, done.shape[0], 8):
        upper = upper_in[t : t + 8, :]
        lower = lower_in[t : t + 8, :]
        for r, back in rounds:
            c = angles_ref[2 * r : 2 * r + 1, :]
            s = angles_ref[2 * r + 1 : 2 * r + 2, :]
            lower = pltpu.roll(lower, back, 1)
            upper, lower = upper * c + lower * s, lower * c - upper * s
        done[t : t + 8, :] = pltpu.roll(lower, shift_ref[shift_ref.shape[0] - 1], 1)
    copy = pltpu.make_async_copy(done, pair_ref.at[:, w:], sem)
    copy.start()
    copy.wait()


def passed_along(block, axis, distance):
    devices = range(lax.axis_size(axis))
    route = [((i - distance) % len(devices), i) for i in devices]
    return lax.ppermute(block, axis, route)


def swapped(block, axis, bits):
    return lax.ppermute(block, axis, [(i, i ^ bits) for i in range(lax.axis_size(axis))])


def within_four(outs, axis):
    sent = [swapped(outs[k], axis, k) for k in (3, 1, 2)]
    return (outs[0] + sent[1]) + (sent[2] + sent[0])


def across_fours(mine, axis):
    met = [swapped(mine, axis, k) for k in (4, 12, 8)]
    return (mine + met[0]) + (met[1] + met[2])


def met_across(mine, axis):
    h = mine.shape[0] // 2 // 8 * 8
    a, b = mine[:h], mine[h:]
    a1, b1 = swapped(a, axis, 4), swapped(b, axis, 12)
    a, b = a + a1, b + b1
    a1, b1 = swapped(a, axis, 12), swapped(b, axis, 4)
    return jnp.concatenate([a + a1, b + b1], axis=0)


def shared_in_four(mine, axis):
    shared = [swapped(mine, axis, k) for k in (3, 1, 2)]
    return (mine, shared[1], shared[2], shared[0])


def per_device(matrix, shifts):
    rows, width = matrix.shape
    w = width // 2
    block = (rows, w)
    square = (w, w)
    diag = (32, w)
    angles = (2 * shifts.shape[1], w)
    place = (lax.axis_index("row") % 4).astype(jnp.int32).reshape(1)

    gram = kernel_call(
        gram_kernel, [(2 * w // 4 + 8, w)] * 4, [SMEM, VMEM], [square, square, diag]
    )(place, matrix)
    sent = [swapped(gram[k], "row", k) for k in (3, 1, 2)]
    sent[2], moved = lax.optimization_barrier((sent[2], matrix))
    other = passed_along(moved, "col", 2)
    gram = (gram[0] + sent[1]) + (sent[2] + sent[0])
    gram = shared_in_four(met_across(gram, "row"), "row")
    here, *state = kernel_call(
        first_kernel, [angles] + [square] * 3, [SMEM, SMEM] + [VMEM] * 4, [diag]
    )(place, shifts[0], *gram)
    there = passed_along(here, "col", 2)
    own_upper, lower = kernel_call(own_kernel, [block, block], [SMEM, VMEM, VMEM])(
        shifts[0], here, matrix
    )
    tl, lr = kernel_call(last_kernel, [(3 * w // 4, w), square], [SMEM] + [VMEM] * 4)(
        shifts[0], here, *state
    )
    upper, *cross = kernel_call(
        cross_kernel,
        [block] + [(w // 4, w)] * 4,
        [SMEM, SMEM] + [VMEM] * 3,
        [block, square],
    )(place, shifts[0], there, other, lower)
    sent = [swapped(cross[k], "row", k) for k in (3, 1, 2)]
    sent[2], tl = lax.optimization_barrier((sent[2], tl))
    cross = (cross[0] + sent[1]) + (sent[2] + sent[0])
    tl = passed_along(tl, "col", 2)
    tl, sent = lax.optimization_barrier((tl, lower))
    far_lower = passed_along(sent, "col", -2)
    cross = shared_in_four(across_fours(cross, "row"), "row")
    (here,) = kernel_call(
        second_kernel, [angles], [SMEM, SMEM] + [VMEM] * 6, [square] * 3
    )(place, shifts[1], *cross, tl, lr)
    there = passed_along(here, "col", -2)
    half = output_call(upper_kernel, matrix, [VMEM] * 3, [block, block])(
        shifts[1], here, upper, lower
    )
    return output_call(lower_kernel, matrix, [VMEM] * 3 + [ANY], [block], {4: 0})(
        shifts[1], there, own_upper, far_lower, half
    )


def solution(mesh):
    in_specs = (P("row", "col"), P())
    out_specs = P("row", "col")
    return jax.shard_map(
        per_device, mesh=mesh, in_specs=in_specs, out_specs=out_specs, check_vma=False
    )
```

```python
import jax
import jax.numpy as jnp
from jax import lax
from jax.experimental import pallas as pl
from jax.experimental.pallas import tpu as pltpu
from jax.sharding import PartitionSpec as P

LANES = 128
BLK = 256
VMEM = pl.BlockSpec(memory_space=pltpu.VMEM)
SMEM = pl.BlockSpec(memory_space=pltpu.SMEM)
ANY = pl.BlockSpec(memory_space=pl.ANY)


def kernel_call(kernel, outs, ins, scratch=()):
    return pl.pallas_call(
        kernel,
        out_shape=[jax.ShapeDtypeStruct(shape, jnp.float32) for shape in outs],
        in_specs=ins,
        out_specs=[VMEM] * len(outs),
        scratch_shapes=[pltpu.VMEM(shape, jnp.float32) for shape in scratch],
        compiler_params=pltpu.CompilerParams(vmem_limit_bytes=32 * 1024 * 1024),
    )


def output_call(kernel, like, ins, scratch, aliases={}):
    return pl.pallas_call(
        kernel,
        out_shape=jax.ShapeDtypeStruct(like.shape, jnp.float32),
        in_specs=[SMEM] + ins,
        out_specs=ANY,
        scratch_shapes=[pltpu.VMEM(shape, jnp.float32) for shape in scratch]
        + [pltpu.SemaphoreType.DMA],
        input_output_aliases=aliases,
        compiler_params=pltpu.CompilerParams(vmem_limit_bytes=32 * 1024 * 1024),
    )


def half_angle(x, y):
    scale = jnp.maximum(jnp.abs(x), jnp.abs(y))
    flat = scale == 0.0
    inverse = 1.0 / jnp.where(flat, 1.0, scale)
    xs = x * inverse
    ys = y * inverse
    norm = lax.rsqrt(jnp.where(flat, 1.0, xs * xs + ys * ys))
    major = jnp.sqrt(0.5 + 0.5 * jnp.abs(xs * norm))
    minor = 0.5 * jnp.abs(ys * norm) / major
    negative = (y < 0.0) | ((y == 0.0) & (1.0 / y < 0.0))
    ahead = x >= 0.0
    cosine = jnp.where(flat, 1.0, jnp.where(ahead, major, minor))
    sine = jnp.where(ahead, minor, major)
    sine = jnp.where(negative, -sine, sine)
    return cosine, jnp.where(flat, 0.0, sine)


def grid_of(w):
    rows = lax.broadcasted_iota(jnp.int32, (w, w), 0)
    cols = lax.broadcasted_iota(jnp.int32, (w, w), 1)
    return rows, cols


def diagonal(block):
    rows, cols = grid_of(LANES)
    parts = [
        jnp.sum(jnp.where(rows == cols, block[t : t + LANES, t : t + LANES], 0.0), 0, keepdims=True)
        for t in range(0, block.shape[0], LANES)
    ]
    return jnp.concatenate(parts, axis=1)


def turned_along(vector, back):
    return pltpu.roll(jnp.broadcast_to(vector, (8, vector.shape[1])), back, 1)[:1]


def as_rows(vector):
    w = vector.shape[1]
    half = jnp.transpose(jnp.broadcast_to(vector, (LANES, w)))
    return jnp.concatenate([half] * (w // LANES), axis=1)


def turns(shift_ref):
    offset = jnp.int32(0)
    for r in range(shift_ref.shape[0]):
        target = shift_ref[r]
        yield r, lax.rem(offset - target + 2 * BLK, BLK)
        offset = target


def inner_rounds(shift_ref, tl, tr, lr, angles_ref, finished_later=False):
    w = tl.shape[0]

    a = diagonal(tl[...])
    b = diagonal(lr[...])
    for r, back in turns(shift_ref):
        top_left = tl[...]
        top_right = pltpu.roll(tr[...], back, 1)
        low_right = pltpu.roll(pltpu.roll(lr[...], back, 1), back, 0)
        g = diagonal(top_right)
        b = turned_along(b, back)
        c, s = half_angle(a - b, 2.0 * g)
        angles_ref[2 * r : 2 * r + 1, :] = c
        angles_ref[2 * r + 1 : 2 * r + 2, :] = s
        a, b = (
            (c * a + s * g) * c + (c * g + s * b) * s,
            (c * b - s * g) * c - (c * g - s * a) * s,
        )
        left = shift_ref.shape[0] - 1 - r
        if left == 0:
            break
        c_rows = as_rows(c)
        s_rows = as_rows(s)
        low_left = jnp.transpose(top_right)
        half_tl = c_rows * top_left + s_rows * low_left
        half_tr = c_rows * top_right + s_rows * low_right
        half_ll = c_rows * low_left - s_rows * top_left
        half_lr = c_rows * low_right - s_rows * top_right
        tr[...] = half_tr * c - half_tl * s
        if left > 1 or finished_later:
            tl[...] = half_tl * c + half_tr * s
            lr[...] = half_lr * c - half_ll * s


def last_update(shift_ref, angles_ref, tl, tr, lr):
    w = tl.shape[0]
    last = shift_ref.shape[0] - 1
    back = lax.rem(shift_ref[last - 1] - shift_ref[last] + 2 * BLK, BLK)
    c = angles_ref[2 * last : 2 * last + 1, :]
    s = angles_ref[2 * last + 1 : 2 * last + 2, :]
    c_rows = as_rows(c)
    s_rows = as_rows(s)
    top_left = tl[...]
    top_right = pltpu.roll(tr[...], back, 1)
    low_left = jnp.transpose(top_right)
    low_right = pltpu.roll(pltpu.roll(lr[...], back, 1), back, 0)
    half_tl = c_rows * top_left + s_rows * low_left
    half_tr = c_rows * top_right + s_rows * low_right
    half_ll = c_rows * low_left - s_rows * top_left
    half_lr = c_rows * low_right - s_rows * top_right
    offset = shift_ref[last]
    low_right = half_lr * c - half_ll * s
    return (
        half_tl * c + half_tr * s,
        pltpu.roll(pltpu.roll(low_right, offset, 1), offset, 0),
    )


def rotated(shift_ref, angles_ref, upper_ref, lower_ref):
    for r, back in turns(shift_ref):
        c = angles_ref[2 * r : 2 * r + 1, :]
        s = angles_ref[2 * r + 1 : 2 * r + 2, :]
        upper = upper_ref[...]
        lower = pltpu.roll(lower_ref[...], back, 1)
        upper_ref[...] = upper * c + lower * s
        lower_ref[...] = lower * c - upper * s
    offset = shift_ref[shift_ref.shape[0] - 1]
    lower_ref[...] = pltpu.roll(lower_ref[...], offset, 1)


def rotated_rows(shift_ref, angles_ref, upper_ref, lower_ref):
    rounds = list(turns(shift_ref))
    for t in range(0, upper_ref.shape[0], 8):
        part = slice(t, t + 8)
        upper = upper_ref[part, :]
        lower = lower_ref[part, :]
        for r, back in rounds:
            c = angles_ref[2 * r : 2 * r + 1, :]
            s = angles_ref[2 * r + 1 : 2 * r + 2, :]
            lower = pltpu.roll(lower, back, 1)
            upper, lower = upper * c + lower * s, lower * c - upper * s
        yield part, upper, pltpu.roll(lower, shift_ref[shift_ref.shape[0] - 1], 1)


def full_dot(left, right):
    return lax.dot_general(
        left,
        right,
        (((0,), (0,)), ((), ())),
        precision=lax.Precision.HIGHEST,
        preferred_element_type=jnp.float32,
    )


def hand_out(place_ref, blocks, outs):
    for k, out in enumerate(outs):
        start = 0
        for block in blocks:
            share = block.shape[0] // len(outs)
            quarter = (place_ref[0] ^ k) * share
            out[start : start + share, :] = block[pl.ds(pl.multiple_of(quarter, 8), share), :]
            start += share


def take_in(place_ref, ins, blocks):
    for k, piece in enumerate(ins):
        start = 0
        for block in blocks:
            share = block.shape[0] // len(ins)
            quarter = (place_ref[0] ^ k) * share
            block[pl.ds(pl.multiple_of(quarter, 8), share), :] = piece[start : start + share, :]
            start += share


def gram_kernel(place_ref, pair_ref, out0, out1, out2, out3, square, cross, diag):
    outs = (out0, out1, out2, out3)
    w = pair_ref.shape[1] // 2
    rows, cols = grid_of(w)
    upper = pair_ref[:, :w]
    lower = pair_ref[:, w:]
    low_right = full_dot(lower, lower)
    square[...] = jnp.where(rows <= cols, full_dot(upper, upper), low_right)
    cross[...] = full_dot(upper, lower)
    diag[...] = jnp.broadcast_to(diagonal(low_right), diag.shape)
    hand_out(place_ref, (square, cross, diag), outs)


def first_kernel(
    place_ref, shift_ref, in0, in1, in2, in3, angles_ref, tl, tr, lr, diag
):
    w = tl.shape[0]
    rows, cols = grid_of(w)
    take_in(place_ref, (in0, in1, in2, in3), (tl, tr, diag))
    square = tl[...]
    turned = jnp.transpose(square)
    lr[...] = jnp.where(rows == cols, diag[:1, :], jnp.where(rows > cols, square, turned))
    tl[...] = jnp.where(rows <= cols, square, turned)
    inner_rounds(shift_ref, tl, tr, lr, angles_ref, finished_later=True)


def last_kernel(shift_ref, angles_ref, tl, tr, lr, tl_ref, lr_ref):
    top_left, lr_ref[...] = last_update(shift_ref, angles_ref, tl, tr, lr)
    tl_ref[...] = packed(top_left)


def own_kernel(shift_ref, angles_ref, pair_ref, upper_ref, lower_ref):
    w = upper_ref.shape[1]
    upper_ref[...] = pair_ref[:, :w]
    lower_ref[...] = pair_ref[:, w:]
    rotated(shift_ref, angles_ref, upper_ref, lower_ref)


def cross_kernel(
    place_ref, shift_ref, angles_ref, other_ref, lower_ref, upper_ref, out0, out1, out2, out3, cross
):
    w = upper_ref.shape[1]
    halves = (other_ref.at[:, :w], other_ref.at[:, w:])
    for part, upper, _ in rotated_rows(shift_ref, angles_ref, *halves):
        upper_ref[part, :] = upper
    cross[...] = full_dot(upper_ref[...], lower_ref[...])
    hand_out(place_ref, (cross,), (out0, out1, out2, out3))


def packed(block):
    h = block.shape[0] // 2
    q = h // 2
    low = block[h:, h:]
    return jnp.concatenate([block[:h], jnp.concatenate([low[:q], low[q:]], axis=1)], axis=0)


def unpacked(parts):
    h = parts.shape[1] // 2
    q = h // 2
    top = parts[:h]
    low = jnp.concatenate([parts[h:, :h], parts[h:, h:]], axis=0)
    low = jnp.concatenate([jnp.transpose(top[:, h:]), low], axis=1)
    return jnp.concatenate([top, low], axis=0)


def second_kernel(place_ref, shift_ref, in0, in1, in2, in3, tl_ref, lr_ref, angles_ref, tl, tr, lr):
    tl[...] = unpacked(tl_ref[...])
    lr[...] = lr_ref[...]
    take_in(place_ref, (in0, in1, in2, in3), (tr,))
    inner_rounds(shift_ref, tl, tr, lr, angles_ref)


def upper_kernel(shift_ref, angles_ref, upper_in, lower_in, pair_ref, upper, rest, sem):
    upper[...] = upper_in[...]
    rest[...] = lower_in[...]
    rotated(shift_ref, angles_ref, upper, rest)
    copy = pltpu.make_async_copy(upper, pair_ref.at[:, : upper.shape[1]], sem)
    copy.start()
    copy.wait()


def lower_kernel(shift_ref, angles_ref, upper_in, lower_in, half_ref, pair_ref, done, sem):
    w = done.shape[1]
    for part, _, lower in rotated_rows(shift_ref, angles_ref, upper_in, lower_in):
        done[part, :] = lower
    copy = pltpu.make_async_copy(done, pair_ref.at[:, w:], sem)
    copy.start()
    copy.wait()


def passed_along(block, axis, distance):
    devices = range(lax.axis_size(axis))
    route = [((i - distance) % len(devices), i) for i in devices]
    return lax.ppermute(block, axis, route)


def swapped(block, axis, bits):
    return lax.ppermute(block, axis, [(i, i ^ bits) for i in range(lax.axis_size(axis))])


def within_four(outs, axis):
    sent = [swapped(outs[k], axis, k) for k in (3, 1, 2)]
    return (outs[0] + sent[1]) + (sent[2] + sent[0])


def across_fours(mine, axis):
    met = [swapped(mine, axis, k) for k in (4, 12, 8)]
    return (mine + met[0]) + (met[1] + met[2])


def met_across(mine, axis):
    h = mine.shape[0] // 2 // 8 * 8
    a, b = mine[:h], mine[h:]
    a1, b1 = swapped(a, axis, 4), swapped(b, axis, 12)
    a, b = a + a1, b + b1
    a1, b1 = swapped(a, axis, 12), swapped(b, axis, 4)
    return jnp.concatenate([a + a1, b + b1], axis=0)


def shared_in_four(mine, axis):
    shared = [swapped(mine, axis, k) for k in (2, 3, 1)]
    return (mine, shared[2], shared[0], shared[1])


def per_device(matrix, shifts):
    rows, width = matrix.shape
    w = width // 2
    block = (rows, w)
    square = (w, w)
    diag = (32, w)
    angles = (2 * shifts.shape[1], w)
    place = (lax.axis_index("row") % 4).astype(jnp.int32).reshape(1)

    gram = kernel_call(
        gram_kernel, [(2 * w // 4 + 8, w)] * 4, [SMEM, VMEM], [square, square, diag]
    )(place, matrix)
    sent = [swapped(gram[k], "row", k) for k in (2, 1, 3)]
    sent[0], moved = lax.optimization_barrier((sent[0], matrix))
    other = passed_along(moved, "col", 2)
    gram = (gram[0] + sent[1]) + (sent[0] + sent[2])
    gram = shared_in_four(met_across(gram, "row"), "row")
    here, *state = kernel_call(
        first_kernel, [angles] + [square] * 3, [SMEM, SMEM] + [VMEM] * 4, [diag]
    )(place, shifts[0], *gram)
    there = passed_along(here, "col", 2)
    own_upper, lower = kernel_call(own_kernel, [block, block], [SMEM, VMEM, VMEM])(
        shifts[0], here, matrix
    )
    tl, lr = kernel_call(last_kernel, [(3 * w // 4, w), square], [SMEM] + [VMEM] * 4)(
        shifts[0], here, *state
    )
    upper, *cross = kernel_call(
        cross_kernel,
        [block] + [(w // 4, w)] * 4,
        [SMEM, SMEM] + [VMEM] * 3,
        [square],
    )(place, shifts[0], there, other, lower)
    sent = [swapped(cross[k], "row", k) for k in (3, 1, 2)]
    sent[2], tl = lax.optimization_barrier((sent[2], tl))
    cross = (cross[0] + sent[1]) + (sent[2] + sent[0])
    tl = passed_along(tl, "col", 2)
    tl, sent = lax.optimization_barrier((tl, lower))
    far_lower = passed_along(sent, "col", -2)
    cross = shared_in_four(across_fours(cross, "row"), "row")
    (here,) = kernel_call(
        second_kernel, [angles], [SMEM, SMEM] + [VMEM] * 6, [square] * 3
    )(place, shifts[1], *cross, tl, lr)
    there = passed_along(here, "col", -2)
    half = output_call(upper_kernel, matrix, [VMEM] * 3, [block, block])(
        shifts[1], here, upper, lower
    )
    return output_call(lower_kernel, matrix, [VMEM] * 3 + [ANY], [block], {4: 0})(
        shifts[1], there, own_upper, far_lower, half
    )


def solution(mesh):
    in_specs = (P("row", "col"), P())
    out_specs = P("row", "col")
    return jax.shard_map(
        per_device, mesh=mesh, in_specs=in_specs, out_specs=out_specs, check_vma=False
    )
```

```python
import jax
import jax.numpy as jnp
from jax import lax
from jax.experimental import pallas as pl
from jax.experimental.pallas import tpu as pltpu
from jax.sharding import PartitionSpec as P

LANES = 128
BLK = 256
VMEM = pl.BlockSpec(memory_space=pltpu.VMEM)
SMEM = pl.BlockSpec(memory_space=pltpu.SMEM)
ANY = pl.BlockSpec(memory_space=pl.ANY)


def kernel_call(kernel, outs, ins, scratch=()):
    return pl.pallas_call(
        kernel,
        out_shape=[jax.ShapeDtypeStruct(shape, jnp.float32) for shape in outs],
        in_specs=ins,
        out_specs=[VMEM] * len(outs),
        scratch_shapes=[pltpu.VMEM(shape, jnp.float32) for shape in scratch],
        compiler_params=pltpu.CompilerParams(vmem_limit_bytes=32 * 1024 * 1024),
    )


def output_call(kernel, like, ins, scratch, aliases={}):
    return pl.pallas_call(
        kernel,
        out_shape=jax.ShapeDtypeStruct(like.shape, jnp.float32),
        in_specs=[SMEM] + ins,
        out_specs=ANY,
        scratch_shapes=[pltpu.VMEM(shape, jnp.float32) for shape in scratch]
        + [pltpu.SemaphoreType.DMA],
        input_output_aliases=aliases,
        compiler_params=pltpu.CompilerParams(vmem_limit_bytes=32 * 1024 * 1024),
    )


def half_angle(x, y):
    scale = jnp.maximum(jnp.abs(x), jnp.abs(y))
    flat = scale == 0.0
    inverse = 1.0 / jnp.where(flat, 1.0, scale)
    xs = x * inverse
    ys = y * inverse
    norm = lax.rsqrt(jnp.where(flat, 1.0, xs * xs + ys * ys))
    major = jnp.sqrt(0.5 + 0.5 * jnp.abs(xs * norm))
    minor = 0.5 * jnp.abs(ys * norm) / major
    negative = (y < 0.0) | ((y == 0.0) & (1.0 / y < 0.0))
    ahead = x >= 0.0
    cosine = jnp.where(flat, 1.0, jnp.where(ahead, major, minor))
    sine = jnp.where(ahead, minor, major)
    sine = jnp.where(negative, -sine, sine)
    return cosine, jnp.where(flat, 0.0, sine)


def grid_of(w):
    rows = lax.broadcasted_iota(jnp.int32, (w, w), 0)
    cols = lax.broadcasted_iota(jnp.int32, (w, w), 1)
    return rows, cols


def diagonal(block):
    rows, cols = grid_of(LANES)
    parts = [
        jnp.sum(jnp.where(rows == cols, block[t : t + LANES, t : t + LANES], 0.0), 0, keepdims=True)
        for t in range(0, block.shape[0], LANES)
    ]
    return jnp.concatenate(parts, axis=1)


def turned_along(vector, back):
    return pltpu.roll(jnp.broadcast_to(vector, (8, vector.shape[1])), back, 1)[:1]


def as_rows(vector):
    w = vector.shape[1]
    half = jnp.transpose(jnp.broadcast_to(vector, (LANES, w)))
    return jnp.concatenate([half] * (w // LANES), axis=1)


def turns(shift_ref):
    offset = jnp.int32(0)
    for r in range(shift_ref.shape[0]):
        target = shift_ref[r]
        yield r, lax.rem(offset - target + 2 * BLK, BLK)
        offset = target


def inner_rounds(shift_ref, tl, tr, lr, angles_ref, finished_later=False):
    w = tl.shape[0]

    a = diagonal(tl[...])
    b = diagonal(lr[...])
    for r, back in turns(shift_ref):
        top_left = tl[...]
        top_right = pltpu.roll(tr[...], back, 1)
        low_right = pltpu.roll(pltpu.roll(lr[...], back, 1), back, 0)
        g = diagonal(top_right)
        b = turned_along(b, back)
        c, s = half_angle(a - b, 2.0 * g)
        angles_ref[2 * r : 2 * r + 1, :] = c
        angles_ref[2 * r + 1 : 2 * r + 2, :] = s
        a, b = (
            (c * a + s * g) * c + (c * g + s * b) * s,
            (c * b - s * g) * c - (c * g - s * a) * s,
        )
        left = shift_ref.shape[0] - 1 - r
        if left == 0:
            break
        c_rows = as_rows(c)
        s_rows = as_rows(s)
        low_left = jnp.transpose(top_right)
        half_tl = c_rows * top_left + s_rows * low_left
        half_tr = c_rows * top_right + s_rows * low_right
        half_ll = c_rows * low_left - s_rows * top_left
        half_lr = c_rows * low_right - s_rows * top_right
        tr[...] = half_tr * c - half_tl * s
        if left > 1 or finished_later:
            tl[...] = half_tl * c + half_tr * s
            lr[...] = half_lr * c - half_ll * s


def last_update(shift_ref, angles_ref, tl, tr, lr):
    w = tl.shape[0]
    last = shift_ref.shape[0] - 1
    back = lax.rem(shift_ref[last - 1] - shift_ref[last] + 2 * BLK, BLK)
    c = angles_ref[2 * last : 2 * last + 1, :]
    s = angles_ref[2 * last + 1 : 2 * last + 2, :]
    c_rows = as_rows(c)
    s_rows = as_rows(s)
    top_left = tl[...]
    top_right = pltpu.roll(tr[...], back, 1)
    low_left = jnp.transpose(top_right)
    low_right = pltpu.roll(pltpu.roll(lr[...], back, 1), back, 0)
    half_tl = c_rows * top_left + s_rows * low_left
    half_tr = c_rows * top_right + s_rows * low_right
    half_ll = c_rows * low_left - s_rows * top_left
    half_lr = c_rows * low_right - s_rows * top_right
    offset = shift_ref[last]
    low_right = half_lr * c - half_ll * s
    return (
        half_tl * c + half_tr * s,
        pltpu.roll(pltpu.roll(low_right, offset, 1), offset, 0),
    )


def rotated(shift_ref, angles_ref, upper_ref, lower_ref):
    for r, back in turns(shift_ref):
        c = angles_ref[2 * r : 2 * r + 1, :]
        s = angles_ref[2 * r + 1 : 2 * r + 2, :]
        upper = upper_ref[...]
        lower = pltpu.roll(lower_ref[...], back, 1)
        upper_ref[...] = upper * c + lower * s
        lower_ref[...] = lower * c - upper * s
    offset = shift_ref[shift_ref.shape[0] - 1]
    lower_ref[...] = pltpu.roll(lower_ref[...], offset, 1)


def rotated_rows(shift_ref, angles_ref, upper_ref, lower_ref):
    rounds = list(turns(shift_ref))
    for t in range(0, upper_ref.shape[0], 8):
        part = slice(t, t + 8)
        upper = upper_ref[part, :]
        lower = lower_ref[part, :]
        for r, back in rounds:
            c = angles_ref[2 * r : 2 * r + 1, :]
            s = angles_ref[2 * r + 1 : 2 * r + 2, :]
            lower = pltpu.roll(lower, back, 1)
            upper, lower = upper * c + lower * s, lower * c - upper * s
        yield part, upper, pltpu.roll(lower, shift_ref[shift_ref.shape[0] - 1], 1)


def full_dot(left, right):
    return lax.dot_general(
        left,
        right,
        (((0,), (0,)), ((), ())),
        precision=lax.Precision.HIGHEST,
        preferred_element_type=jnp.float32,
    )


def hand_out(place_ref, blocks, outs):
    for k, out in enumerate(outs):
        start = 0
        for block in blocks:
            share = block.shape[0] // len(outs)
            quarter = (place_ref[0] ^ k) * share
            out[start : start + share, :] = block[pl.ds(pl.multiple_of(quarter, 8), share), :]
            start += share


def take_in(place_ref, ins, blocks):
    for k, piece in enumerate(ins):
        start = 0
        for block in blocks:
            share = block.shape[0] // len(ins)
            quarter = (place_ref[0] ^ k) * share
            block[pl.ds(pl.multiple_of(quarter, 8), share), :] = piece[start : start + share, :]
            start += share


def gram_kernel(place_ref, pair_ref, out0, out1, out2, out3, square, cross, diag):
    outs = (out0, out1, out2, out3)
    w = pair_ref.shape[1] // 2
    rows, cols = grid_of(w)
    upper = pair_ref[:, :w]
    lower = pair_ref[:, w:]
    low_right = full_dot(lower, lower)
    square[...] = jnp.where(rows <= cols, full_dot(upper, upper), low_right)
    cross[...] = full_dot(upper, lower)
    diag[...] = jnp.broadcast_to(diagonal(low_right), diag.shape)
    hand_out(place_ref, (square, cross, diag), outs)


def first_kernel(
    place_ref, shift_ref, in0, in1, in2, in3, angles_ref, tl, tr, lr, diag
):
    w = tl.shape[0]
    rows, cols = grid_of(w)
    take_in(place_ref, (in0, in1, in2, in3), (tl, tr, diag))
    square = tl[...]
    turned = jnp.transpose(square)
    lr[...] = jnp.where(rows == cols, diag[:1, :], jnp.where(rows > cols, square, turned))
    tl[...] = jnp.where(rows <= cols, square, turned)
    inner_rounds(shift_ref, tl, tr, lr, angles_ref, finished_later=True)


def last_kernel(shift_ref, angles_ref, tl, tr, lr, tl_ref, lr_ref):
    top_left, lr_ref[...] = last_update(shift_ref, angles_ref, tl, tr, lr)
    tl_ref[...] = packed(top_left)


def own_kernel(shift_ref, angles_ref, pair_ref, upper_ref, lower_ref):
    w = upper_ref.shape[1]
    upper_ref[...] = pair_ref[:, :w]
    lower_ref[...] = pair_ref[:, w:]
    rotated(shift_ref, angles_ref, upper_ref, lower_ref)


def cross_kernel(
    place_ref, shift_ref, angles_ref, other_ref, lower_ref, upper_ref, out0, out1, out2, out3, cross
):
    w = upper_ref.shape[1]
    halves = (other_ref.at[:, :w], other_ref.at[:, w:])
    for part, upper, _ in rotated_rows(shift_ref, angles_ref, *halves):
        upper_ref[part, :] = upper
    cross[...] = full_dot(upper_ref[...], lower_ref[...])
    hand_out(place_ref, (cross,), (out0, out1, out2, out3))


def packed(block):
    h = block.shape[0] // 2
    q = h // 2
    low = block[h:, h:]
    return jnp.concatenate([block[:h], jnp.concatenate([low[:q], low[q:]], axis=1)], axis=0)


def unpacked(parts):
    h = parts.shape[1] // 2
    q = h // 2
    top = parts[:h]
    low = jnp.concatenate([parts[h:, :h], parts[h:, h:]], axis=0)
    low = jnp.concatenate([jnp.transpose(top[:, h:]), low], axis=1)
    return jnp.concatenate([top, low], axis=0)


def second_kernel(place_ref, shift_ref, in0, in1, in2, in3, tl_ref, lr_ref, angles_ref, tl, tr, lr):
    tl[...] = unpacked(tl_ref[...])
    lr[...] = lr_ref[...]
    take_in(place_ref, (in0, in1, in2, in3), (tr,))
    inner_rounds(shift_ref, tl, tr, lr, angles_ref)


def upper_kernel(shift_ref, angles_ref, upper_in, lower_in, pair_ref, upper, rest, sem):
    upper[...] = upper_in[...]
    rest[...] = lower_in[...]
    rotated(shift_ref, angles_ref, upper, rest)
    copy = pltpu.make_async_copy(upper, pair_ref.at[:, : upper.shape[1]], sem)
    copy.start()
    copy.wait()


def lower_kernel(shift_ref, angles_ref, upper_in, lower_in, half_ref, pair_ref, done, sem):
    w = done.shape[1]
    for part, _, lower in rotated_rows(shift_ref, angles_ref, upper_in, lower_in):
        done[part, :] = lower
    copy = pltpu.make_async_copy(done, pair_ref.at[:, w:], sem)
    copy.start()
    copy.wait()


def passed_along(block, axis, distance):
    devices = range(lax.axis_size(axis))
    route = [((i - distance) % len(devices), i) for i in devices]
    return lax.ppermute(block, axis, route)


def swapped(block, axis, bits):
    return lax.ppermute(block, axis, [(i, i ^ bits) for i in range(lax.axis_size(axis))])


def within_four(outs, axis):
    sent = [swapped(outs[k], axis, k) for k in (3, 1, 2)]
    return (outs[0] + sent[1]) + (sent[2] + sent[0])


def across_fours(mine, axis):
    met = [swapped(mine, axis, k) for k in (4, 12, 8)]
    return (mine + met[0]) + (met[1] + met[2])


def met_across(mine, axis):
    h = mine.shape[0] // 2 // 8 * 8
    a, b = mine[:h], mine[h:]
    a1, b1 = swapped(a, axis, 4), swapped(b, axis, 12)
    a, b = a + a1, b + b1
    a1, b1 = swapped(a, axis, 12), swapped(b, axis, 4)
    return jnp.concatenate([a + a1, b + b1], axis=0)


def shared_in_four(mine, axis):
    shared = [swapped(mine, axis, k) for k in (2, 3, 1)]
    return (mine, shared[2], shared[0], shared[1])


def per_device(matrix, shifts):
    rows, width = matrix.shape
    w = width // 2
    block = (rows, w)
    square = (w, w)
    diag = (32, w)
    angles = (2 * shifts.shape[1], w)
    place = (lax.axis_index("row") % 4).astype(jnp.int32).reshape(1)

    gram = kernel_call(
        gram_kernel, [(2 * w // 4 + 8, w)] * 4, [SMEM, VMEM], [square, square, diag]
    )(place, matrix)
    sent = [swapped(gram[k], "row", k) for k in (2, 1, 3)]
    sent[0], moved = lax.optimization_barrier((sent[0], matrix))
    other = passed_along(moved, "col", 2)
    gram = (gram[0] + sent[1]) + (sent[0] + sent[2])
    gram = shared_in_four(met_across(gram, "row"), "row")
    here, *state = kernel_call(
        first_kernel, [angles] + [square] * 3, [SMEM, SMEM] + [VMEM] * 4, [diag]
    )(place, shifts[0], *gram)
    there = passed_along(here, "col", 2)
    own_upper, lower = kernel_call(own_kernel, [block, block], [SMEM, VMEM, VMEM])(
        shifts[0], here, matrix
    )
    tl, lr = kernel_call(last_kernel, [(3 * w // 4, w), square], [SMEM] + [VMEM] * 4)(
        shifts[0], here, *state
    )
    upper, *cross = kernel_call(
        cross_kernel,
        [block] + [(w // 4, w)] * 4,
        [SMEM, SMEM] + [VMEM] * 3,
        [square],
    )(place, shifts[0], there, other, lower)
    sent = [swapped(cross[k], "row", k) for k in (2, 1, 3)]
    sent[0], tl = lax.optimization_barrier((sent[0], tl))
    cross = (cross[0] + sent[1]) + (sent[0] + sent[2])
    tl = passed_along(tl, "col", 2)
    tl, sent = lax.optimization_barrier((tl, lower))
    far_lower = passed_along(sent, "col", -2)
    cross = shared_in_four(across_fours(cross, "row"), "row")
    (here,) = kernel_call(
        second_kernel, [angles], [SMEM, SMEM] + [VMEM] * 6, [square] * 3
    )(place, shifts[1], *cross, tl, lr)
    there = passed_along(here, "col", -2)
    half = output_call(upper_kernel, matrix, [VMEM] * 3, [block, block])(
        shifts[1], here, upper, lower
    )
    return output_call(lower_kernel, matrix, [VMEM] * 3 + [ANY], [block], {4: 0})(
        shifts[1], there, own_upper, far_lower, half
    )


def solution(mesh):
    in_specs = (P("row", "col"), P())
    out_specs = P("row", "col")
    return jax.shard_map(
        per_device, mesh=mesh, in_specs=in_specs, out_specs=out_specs, check_vma=False
    )
```
